32 devices in a mesh: grp: 2 (over x), freq: 8 (over z, y), src: 2 (over core).
Axes of the slice: x: 2, y: 2, z: 4, core: 2. Of those that a mesh axis runs over, the one named last changes fastest.
Arguments:
- kernel: bfloat16 [4, 64, 320, 8192], P('grp', 'freq', None, 'src'), parts along dimension 0, may hold values from -0.0625 to 0.0625
- data: float32 [4, 64, 320, 8], P('grp', 'freq'), parts along dimension 0, may hold values from -300 to 300
- win_start: int32 [16], P('grp'), parts along dimension 0, may hold values from 0 to 31
- win_end: int32 [16], P('grp'), parts along dimension 0, may hold values from 64 to 128
Outputs:
- estimate: float32 [4, 64, 8, 8192], P('grp', 'freq', None, 'src'), parts along dimension 0
- residual: float32 [4, 64, 320, 8], P('grp', 'freq', 'src'), parts along dimension 0
The draws below stay inside these ranges and needn't reach their ends.
There are 2 independent parts, one for each index of `grp`. The reference program is written for one: setup_inputs(seed, part) draws one part's arguments, and reference() takes and returns one part's arrays. A program takes and returns all parts, laid end to end along the dimension named above; each array names one. Nothing has to cross between parts.
All inputs are finite; a program needn't handle non-finite values.
Results may differ from the reference program's by a relative error of at most 0.006.
Values may be sent and summed in bfloat16 or wider, within the bound.
No kernel may reach another device: no remote copies, remote signals or barrier semaphores. Data moves between devices by JAX's collectives and lax.ppermute only.
A program may use at most 128 MiB of HBM per device.

```python
import math
import jax
import jax.numpy as jnp
from jax import lax

F = 64
R = 320
S = 8192
ITERS = 2
V = 8
NT = 128


def draw_data(key, part):
    key = jax.random.fold_in(key, 11)
    keys = jax.random.split(key, 3)
    ramp = jnp.exp(math.log(3.0) * jnp.arange(F, dtype=jnp.float32) / (F - 1))
    ramp = ramp * jax.random.uniform(keys[1], (F,), jnp.float32, 0.7, 1.3)
    point_scale = jnp.exp(jax.random.uniform(keys[2], (V,), jnp.float32, math.log(0.3), math.log(3.0)))
    scales = ramp[None, :, None, None] * point_scale[None, None, None, :]
    values = jnp.clip(jax.random.normal(keys[0], (2, F, R, V), jnp.float32), -6.0, 6.0)
    return (values * scales).astype(jnp.float32)


def touch_ends(values, stream_key, low, top_value):
    longest = values.shape.index(max(values.shape))
    spots = []
    for shift in (0, 1):
        where = [jax.random.randint(jax.random.fold_in(stream_key, axis), (), 0, length) for axis, length in enumerate(values.shape)]
        where[longest] = (where[longest] + shift) % values.shape[longest]
        spots.append(tuple(where))
    return values.at[spots[0]].set(low).at[spots[1]].set(top_value)


def level_of(rng, extent, cuts, least, high):
    gain, own = 1.0, jax.random.fold_in(rng, 6)
    for axis_at, blocks in cuts:
        steps = jnp.exp(jax.random.uniform(jax.random.fold_in(own, axis_at), (blocks,), jnp.float32, least / len(cuts), high / len(cuts)))
        gain = gain * jnp.repeat(steps, extent[axis_at] // blocks).reshape([-1 if axis == axis_at else 1 for axis in range(len(extent))])
    return gain


def centred(rng, extent, width, limit, cuts=(), kind=jnp.bfloat16):
    result = jax.random.normal(rng, extent, jnp.float32) * width
    if len(cuts) > 0:
        result = level_of(rng, extent, cuts, -0.22, 0.18) * result
    return jnp.clip(result, min=-limit, max=limit).astype(kind)


def setup_inputs(seed: int = 0, part: int = 0) -> dict:
    key_list = jax.random.split(jax.random.key(seed), 5)
    own_keys = jax.random.split(jax.random.fold_in(key_list[4], part), 5)
    return {
        "kernel": centred(own_keys[0], (2, F, R, S), S ** -0.5, 0.0625, ((1, 8), (3, 2))),
        "data": draw_data(jax.random.fold_in(jax.random.fold_in(key_list[4], part), 71), part),
        "win_start": touch_ends(jax.random.randint(own_keys[2], (V,), 0, NT // 4), jax.random.fold_in(own_keys[2], 1), 0, (NT // 4) - 1).astype(jnp.int32),
        "win_end": touch_ends(jax.random.randint(own_keys[3], (V,), NT // 2, NT + 1), jax.random.fold_in(own_keys[3], 1), NT // 2, NT).astype(jnp.int32),
    }


def window_mask(starts, ends):
    samples = jnp.arange(NT, dtype=jnp.int32)[:, None]
    inside = (samples >= starts[None, :]) & (samples < ends[None, :])
    return inside.astype(jnp.float32)


def sine_tables():
    samples = jnp.arange(NT, dtype=jnp.int32)[:, None]
    freqs = jnp.arange(F, dtype=jnp.int32)[None, :]
    phase = ((samples * freqs) % NT).astype(jnp.float32) * (2.0 * math.pi / NT)
    return jnp.cos(phase), jnp.sin(phase)


def apply_taper(gradient, window):
    cos_table, sin_table = sine_tables()
    norm_scale = F ** -0.5
    highest = lax.Precision.HIGHEST
    signal = norm_scale * (jnp.einsum("tf,fvs->tvs", cos_table, gradient[0], precision=highest)
                           - jnp.einsum("tf,fvs->tvs", sin_table, gradient[1], precision=highest))
    signal = signal * window[:, :, None]
    real_part = norm_scale * jnp.einsum("tf,tvs->fvs", cos_table, signal, precision=highest)
    imag_part = -norm_scale * jnp.einsum("tf,tvs->fvs", sin_table, signal, precision=highest)
    return jnp.stack([real_part, imag_part])


def adjoint_one(kernel_f, resid_f):
    real_part = jnp.dot(resid_f[0].T, kernel_f[0], preferred_element_type=jnp.float32) + jnp.dot(resid_f[1].T, kernel_f[1], preferred_element_type=jnp.float32)
    imag_part = jnp.dot(resid_f[1].T, kernel_f[0], preferred_element_type=jnp.float32) - jnp.dot(resid_f[0].T, kernel_f[1], preferred_element_type=jnp.float32)
    return jnp.stack([real_part, imag_part])


def forward_one(kernel_f, field_f):
    real_part = jnp.dot(kernel_f[0], field_f[0].T, preferred_element_type=jnp.float32) - jnp.dot(kernel_f[1], field_f[1].T, preferred_element_type=jnp.float32)
    imag_part = jnp.dot(kernel_f[0], field_f[1].T, preferred_element_type=jnp.float32) + jnp.dot(kernel_f[1], field_f[0].T, preferred_element_type=jnp.float32)
    return jnp.stack([real_part, imag_part])


def reference(kernel, data, win_start, win_end):
    window = window_mask(win_start, win_end)
    indices = jnp.arange(F, dtype=jnp.int32)
    estimate = jnp.zeros((2, F, V, S), jnp.float32)
    residual = data
    for iteration in range(ITERS):
        resid_b = residual.astype(jnp.bfloat16)
        gradient = jnp.moveaxis(lax.map(lambda index: adjoint_one(kernel[:, index], resid_b[:, index]), indices), 0, 1)
        direction = apply_taper(gradient, window)
        direction_b = direction.astype(jnp.bfloat16)
        projected = jnp.moveaxis(lax.map(lambda index: forward_one(kernel[:, index], direction_b[:, index]), indices), 0, 1)
        alignment = jnp.sum(gradient * direction)
        curvature = jnp.sum(projected * projected)
        step_length = alignment / curvature
        estimate = estimate + step_length * direction
        residual = residual - step_length * projected
    return estimate, residual
```

```python
import functools
import math

import jax
import jax.numpy as jnp
import numpy as np
from jax import lax
from jax.experimental import pallas as pl
from jax.experimental.pallas import tpu as pltpu
from jax.sharding import PartitionSpec as P

ITERS = 2
NT = 128
LANES = 128
BF16 = jnp.bfloat16
F32 = jnp.float32
VMEM_LIMIT = 56 * 2**20
CHUNKS = 2
TILE = 2048
DEPTH = 4


def in_vmem():
    return pl.BlockSpec(memory_space=pltpu.VMEM)


def stream(k_hbm, kbuf, sem, base, steps, fl, step):
    depth, _, _, ts = kbuf.shape
    total = steps * fl

    def copy(i):
        off = pl.multiple_of(base + i // fl * ts, LANES)
        slot = i % depth
        return pltpu.make_async_copy(k_hbm.at[:, i % fl, :, pl.ds(off, ts)], kbuf.at[slot], sem.at[slot])

    for i in range(min(depth - 1, total)):
        copy(i).start()

    def body(i, carry):
        @pl.when(i + depth - 1 < total)
        def _():
            copy(i + depth - 1).start()

        copy(i).wait()
        step(i // fl, i % fl, kbuf.at[i % depth])
        return carry

    lax.fori_loop(0, total, body, 0)


def adjoint_body(l_ref, k_hbm, o_ref, kbuf, sem, scr, *, fl, points, base, steps):
    _, _, receivers, ts = kbuf.shape

    def step(s, f, block):
        out = jnp.dot(l_ref[f], block[...].reshape(2 * receivers, ts), preferred_element_type=F32)
        for c in range(2):
            for j in range(ts // LANES):
                scr[j, pl.ds(c * fl + f, points, stride=2 * fl), :] = out[
                    c * points : (c + 1) * points, j * LANES : (j + 1) * LANES
                ]

        @pl.when(f == fl - 1)
        def _():
            for j in range(ts // LANES):
                o_ref[:, pl.ds(pl.multiple_of(s * ts + j * LANES, LANES), LANES)] = scr[j].astype(BF16)

    stream(k_hbm, kbuf, sem, base, steps, fl, step)


def adjoint(kernel, rows, chunk):
    _, fl, receivers, sources = kernel.shape
    points = rows.shape[1] // 2
    width = sources // CHUNKS
    ts = min(TILE, width)
    return pl.pallas_call(
        functools.partial(adjoint_body, fl=fl, points=points, base=chunk * width, steps=width // ts),
        in_specs=[in_vmem(), pl.BlockSpec(memory_space=pl.ANY)],
        out_specs=in_vmem(),
        out_shape=jax.ShapeDtypeStruct((2 * points * fl, width), BF16),
        scratch_shapes=[
            pltpu.VMEM((DEPTH, 2, receivers, ts), BF16),
            pltpu.SemaphoreType.DMA((DEPTH,)),
            pltpu.VMEM((ts // LANES, 2 * points * fl, LANES), F32),
        ],
        compiler_params=pltpu.CompilerParams(vmem_limit_bytes=VMEM_LIMIT),
        cost_estimate=pl.CostEstimate(
            flops=64 * points * receivers * width * fl, bytes_accessed=4 * fl * receivers * width, transcendentals=0
        ),
        name="adjoint",
    )(rows, kernel)


def forward_body(d_ref, k_hbm, init_ref, al_ref, o_ref, dt_ref, kbuf, sem, dscr, acc, *, fl, points, base, steps):
    _, _, receivers, ts = kbuf.shape
    acc[...] = jnp.zeros(acc.shape, F32)

    def step(s, f, block):
        @pl.when(f == 0)
        def _():
            for j in range(ts // LANES):
                dscr[j] = d_ref[:, pl.ds(pl.multiple_of(s * ts + j * LANES, LANES), LANES)].astype(F32)

        tiles = range(ts // LANES)
        real = jnp.concatenate([dscr[j, pl.ds(f, points, stride=2 * fl), :] for j in tiles], 1)
        imag = jnp.concatenate([dscr[j, pl.ds(fl + f, points, stride=2 * fl), :] for j in tiles], 1)
        at = pl.ds(pl.multiple_of(s * ts, LANES), ts)
        dt_ref[0, f, :, at] = real
        dt_ref[1, f, :, at] = imag
        field = jnp.concatenate([real, imag], 0).astype(BF16)
        acc[f] += lax.dot_general(
            field,
            block[...].reshape(2 * receivers, ts),
            (((1,), (1,)), ((), ())),
            preferred_element_type=F32,
        )

    stream(k_hbm, kbuf, sem, base, steps, fl, step)
    for f in range(fl):
        part = acc[f]
        top = 2 * points * f
        mid = top + points
        end = top + 2 * points
        real = part[:points, :receivers] - part[points:, receivers:]
        imag = part[points:, :receivers] + part[:points, receivers:]
        if init_ref is not None:
            real += init_ref[top:mid]
            imag += init_ref[mid:end]
        o_ref[top:mid] = real
        o_ref[mid:end] = imag
    rest = jnp.zeros((8, receivers - LANES), F32)
    extra = jnp.concatenate([al_ref[...], rest], 1)
    if init_ref is not None:
        extra += init_ref[2 * points * fl :]
    o_ref[2 * points * fl :] = extra


def forward(kernel, field, alignment, init, chunk):
    _, fl, receivers, sources = kernel.shape
    points = field.shape[0] // (2 * fl)
    width = sources // CHUNKS
    ts = min(TILE, width)
    body = functools.partial(forward_body, fl=fl, points=points, base=chunk * width, steps=width // ts)
    args = [field, kernel, alignment]
    if init is None:
        inner = body
        body = lambda d, k, al, *rest: inner(d, k, None, al, *rest)
    else:
        args.insert(2, init)
    specs = [in_vmem(), pl.BlockSpec(memory_space=pl.ANY)] + [in_vmem()] * (len(args) - 2)
    return pl.pallas_call(
        body,
        in_specs=specs,
        out_specs=[in_vmem()] * 2,
        out_shape=[
            jax.ShapeDtypeStruct((2 * points * fl + 8, receivers), F32),
            jax.ShapeDtypeStruct((2, fl, points, width), F32),
        ],
        scratch_shapes=[
            pltpu.VMEM((DEPTH, 2, receivers, ts), BF16),
            pltpu.SemaphoreType.DMA((DEPTH,)),
            pltpu.VMEM((ts // LANES, 2 * points * fl, LANES), F32),
            pltpu.VMEM((fl, 2 * points, 2 * receivers), F32),
        ],
        compiler_params=pltpu.CompilerParams(vmem_limit_bytes=VMEM_LIMIT),
        cost_estimate=pl.CostEstimate(
            flops=64 * points * receivers * width * fl, bytes_accessed=4 * fl * receivers * width, transcendentals=0
        ),
        name="forward",
    )(*args)


def taper_body(t_ref, g_ref, d_ref, al_ref):
    whole = t_ref[...]
    high = whole.astype(BF16)
    rest = whole - high.astype(F32)
    mid = rest.astype(BF16)
    low = (rest - mid.astype(F32)).astype(BF16)
    size, width = g_ref.shape
    step = min(512, width)
    total = jnp.zeros((8, LANES), F32)
    for at in range(0, width, step):
        g = g_ref[:, at : at + step]
        d = jnp.dot(low, g, preferred_element_type=F32)
        d += jnp.dot(mid, g, preferred_element_type=F32)
        d += jnp.dot(high, g, preferred_element_type=F32)
        d_ref[:, at : at + step] = d.astype(BF16)
        product = d * g.astype(F32)
        for j in range(0, step, LANES):
            total += product[:, j : j + LANES].reshape(size // 8, 8, LANES).sum(0)
    al_ref[...] = total


def taper(matrix, gradient):
    size, width = gradient.shape
    return pl.pallas_call(
        taper_body,
        in_specs=[in_vmem()] * 2,
        out_specs=[in_vmem()] * 2,
        out_shape=[jax.ShapeDtypeStruct((size, width), BF16), jax.ShapeDtypeStruct((8, LANES), F32)],
        compiler_params=pltpu.CompilerParams(vmem_limit_bytes=VMEM_LIMIT),
        cost_estimate=pl.CostEstimate(flops=6 * size * size * width, bytes_accessed=4 * size * width, transcendentals=0),
        name="taper",
    )(matrix, gradient)


def wave_table(freqs, fl):
    samples = np.arange(NT)[:, None]
    phase = (samples * np.arange(freqs)[None, :] % NT) * (2.0 * math.pi / NT)
    table = np.stack([np.cos(phase), -np.sin(phase)], 1) * freqs**-0.5
    table = table.reshape(NT, 2, freqs // fl, fl).transpose(0, 2, 1, 3)
    return table.reshape(NT, 2 * freqs).astype(np.float32)


def swap(x):
    return lax.ppermute(x, "src", [(0, 1), (1, 0)])


def total_over(x, axis):
    size = lax.axis_size(axis)
    if size & (size - 1):
        return lax.psum(x, axis)
    hop = 1
    while hop < size:
        x = x + lax.ppermute(x, axis, [(i, i ^ hop) for i in range(size)])
        hop *= 2
    return x


def exchange(x, rows):
    width = x.shape[-1]
    return lax.all_to_all(x.reshape(-1, rows, width), "freq", 0, 0, tiled=True).reshape(-1, width)


def body(kernel, data, win_start, win_end):
    count = lax.axis_size("freq")
    src_count = lax.axis_size("src")
    _, fl, receivers, sources = kernel.shape
    points = data.shape[3]
    own = points // count
    freqs = fl * count
    first = lax.axis_index("freq") * own
    samples = jnp.arange(NT, dtype=jnp.int32)[:, None]
    table = jnp.asarray(wave_table(freqs, fl))
    matrices = []
    for p in range(own):
        start = lax.dynamic_index_in_dim(win_start, first + p, keepdims=False)
        end = lax.dynamic_index_in_dim(win_end, first + p, keepdims=False)
        window = ((samples >= start) & (samples < end)).astype(F32)
        matrices.append(jnp.dot(table.T, window * table, precision=lax.Precision.HIGHEST))

    residual = data.transpose(1, 0, 3, 2).reshape(fl, 2 * points, receivers)
    steps, fields = [], []
    for iteration in range(ITERS):
        rounded = residual.astype(BF16)
        real, imag = rounded[:, :points], rounded[:, points:]
        rows = jnp.concatenate(
            [jnp.concatenate([real, imag], 1), jnp.concatenate([imag, -real], 1)], 2
        )
        image = None
        parts = []
        for chunk in range(CHUNKS):
            gradient = exchange(adjoint(kernel, rows, chunk), 2 * fl)
            width = gradient.shape[-1]
            if own == 1:
                direction, alignment = taper(matrices[0], gradient)
            else:
                blocks = gradient.reshape(count, own, 2 * fl, width)
                done = [taper(matrices[p], blocks[:, p].reshape(-1, width)) for p in range(own)]
                direction = jnp.stack([d.reshape(count, 2 * fl, width) for d, _ in done], 1).reshape(-1, width)
                alignment = sum(a for _, a in done)
            image, part = forward(kernel, exchange(direction, 2 * fl), alignment, image, chunk)
            parts.append(part)
        image = image + (swap(image) if src_count == 2 else lax.psum(image, "src") - image)
        projected = image[:-8].reshape(fl, 2 * points, receivers)
        sums = jnp.stack([jnp.sum(image[-8:]), jnp.sum(projected * projected)])
        sums = total_over(sums, "freq")
        step_length = sums[0] / sums[1]
        residual = residual - step_length * projected
        steps.append(step_length)
        fields.append(parts)
    estimate = jnp.concatenate(
        [sum(s * part for s, part in zip(steps, column)) for column in zip(*fields)], 3
    )
    share = receivers // src_count
    residual = lax.dynamic_slice_in_dim(residual, lax.axis_index("src") * share, share, 2)
    residual = residual.reshape(fl, 2, points, share).transpose(1, 0, 3, 2)
    return estimate, residual


def solution(mesh):
    in_specs = (P("grp", "freq", None, "src"), P("grp", "freq", None, None), P("grp"), P("grp"))
    out_specs = (P("grp", "freq", None, "src"), P("grp", "freq", "src", None))
    return jax.shard_map(body, mesh=mesh, in_specs=in_specs, out_specs=out_specs, check_vma=False)
```

```python
import functools
import math

import jax
import jax.numpy as jnp
import numpy as np
from jax import lax
from jax.experimental import pallas as pl
from jax.experimental.pallas import tpu as pltpu
from jax.sharding import PartitionSpec as P

ITERS = 2
NT = 128
LANES = 128
BF16 = jnp.bfloat16
F32 = jnp.float32
VMEM_LIMIT = 56 * 2**20
PARTS = ((1, "relay"), (1, "relay"))
ADJOINT_TILE = 2048
ADJOINT_DEPTH = 9
FORWARD_TILE = 2048
FORWARD_DEPTH = 9
FORWARD_GROUP = 1
EARLY = False
TIE = 1
TIE2 = True


def in_vmem():
    return pl.BlockSpec(memory_space=pltpu.VMEM)


def tile_of(width, limit):
    return max(t for t in range(LANES, min(limit, width) + 1, LANES) if width % t == 0)


def stream(k_hbm, kbuf, sem, base, steps, step):
    depth, _, group, _, ts = kbuf.shape
    groups = k_hbm.shape[1] // group
    total = steps * groups

    def copy(i):
        off = pl.multiple_of(base + i // groups * ts, LANES)
        slot = i % depth
        source = k_hbm.at[:, pl.ds(i % groups * group, group), :, pl.ds(off, ts)]
        return pltpu.make_async_copy(source, kbuf.at[slot], sem.at[slot])

    for i in range(min(depth - 1, total)):
        copy(i).start()

    def body(i, carry):
        @pl.when(i + depth - 1 < total)
        def _():
            copy(i + depth - 1).start()

        copy(i).wait()
        step(i // groups, i % groups, kbuf.at[i % depth])
        return carry

    lax.fori_loop(0, total, body, 0)


def adjoint_body(turn_ref, l_ref, k_hbm, *refs, points, base, steps):
    *o_refs, kbuf, sem, scr = refs
    _, _, _, receivers, ts = kbuf.shape
    fl = k_hbm.shape[1]
    size = 2 * points * fl // len(o_refs)
    turn = turn_ref[0]

    def step(s, f, block):
        out = jnp.dot(l_ref[f], block[...].reshape(2 * receivers, ts), preferred_element_type=F32)
        for c in range(2):
            for j in range(ts // LANES):
                scr[j, pl.ds(c * fl + f, points, stride=2 * fl), :] = out[
                    c * points : (c + 1) * points, j * LANES : (j + 1) * LANES
                ]

        @pl.when(f == fl - 1)
        def _():
            for k, o_ref in enumerate(o_refs):
                rows = pl.ds(pl.multiple_of((turn ^ k) * size, size), size)
                for j in range(ts // LANES):
                    at = pl.ds(pl.multiple_of(s * ts + j * LANES, LANES), LANES)
                    o_ref[:, at] = scr[j, rows, :].astype(BF16)

    stream(k_hbm, kbuf, sem, base, steps, step)


def adjoint(turn, kernel, rows, base, width, pieces):
    _, fl, receivers, sources = kernel.shape
    points = rows.shape[1] // 2
    ts = tile_of(width, ADJOINT_TILE)
    depth = min(ADJOINT_DEPTH, width // ts * fl)
    return pl.pallas_call(
        functools.partial(adjoint_body, points=points, base=base, steps=width // ts),
        in_specs=[pl.BlockSpec(memory_space=pltpu.SMEM), in_vmem(), pl.BlockSpec(memory_space=pl.ANY)],
        out_specs=[in_vmem()] * pieces,
        out_shape=[jax.ShapeDtypeStruct((2 * points * fl // pieces, width), BF16)] * pieces,
        scratch_shapes=[
            pltpu.VMEM((depth, 2, 1, receivers, ts), BF16),
            pltpu.SemaphoreType.DMA((depth,)),
            pltpu.VMEM((ts // LANES, 2 * points * fl, LANES), F32),
        ],
        compiler_params=pltpu.CompilerParams(vmem_limit_bytes=VMEM_LIMIT),
        cost_estimate=pl.CostEstimate(
            flops=64 * points * receivers * width * fl, bytes_accessed=4 * fl * receivers * width, transcendentals=0
        ),
        name="adjoint",
    )(turn, rows, kernel)


def forward_body(turn_ref, k_hbm, al_ref, init_ref, *refs, pieces, points, base, steps):
    d_refs, (o_ref, kbuf, sem, dscr, acc) = refs[:pieces], refs[pieces:]
    _, _, group, receivers, ts = kbuf.shape
    fl = k_hbm.shape[1]
    size = 2 * points * fl // pieces
    turn = turn_ref[0]
    acc[...] = jnp.zeros(acc.shape, F32)

    def step(s, n, block):
        tiles = range(ts // LANES)

        @pl.when(n == 0)
        def _():
            for k, d_ref in enumerate(d_refs):
                rows = pl.ds(pl.multiple_of((turn ^ k) * size, size), size)
                for j in tiles:
                    at = pl.ds(pl.multiple_of(s * ts + j * LANES, LANES), LANES)
                    dscr[j, rows, :] = d_ref[:, at].astype(F32)

        def part(c, f):
            rows = pl.ds(c * fl + n * group + f, points, stride=2 * fl)
            return jnp.concatenate([dscr[j, rows, :] for j in tiles], 1)

        field = jnp.concatenate([part(c, f) for f in range(group) for c in range(2)], 0).astype(BF16)
        acc[n] += lax.dot_general(
            field,
            block[...].reshape(2 * group * receivers, ts),
            (((1,), (1,)), ((), ())),
            preferred_element_type=F32,
        )

    stream(k_hbm, kbuf, sem, base, steps, step)
    for f in range(fl):
        n, g = divmod(f, group)
        whole = acc[n, 2 * points * g : 2 * points * (g + 1)]
        by_real = whole[:, g * receivers : (g + 1) * receivers]
        by_imag = whole[:, (group + g) * receivers : (group + g + 1) * receivers]
        top = 2 * points * f
        mid = top + points
        end = top + 2 * points
        real = by_real[:points] - by_imag[points:]
        imag = by_real[points:] + by_imag[:points]
        if init_ref is not None:
            real += init_ref[top:mid]
            imag += init_ref[mid:end]
        o_ref[top:mid] = real
        o_ref[mid:end] = imag
    extra = jnp.concatenate([al_ref[...], jnp.zeros((8, receivers - LANES), F32)], 1)
    if init_ref is not None:
        extra += init_ref[2 * points * fl :]
    o_ref[2 * points * fl :] = extra


def forward(turn, kernel, field, alignment, init, base):
    _, fl, receivers, sources = kernel.shape
    pieces = len(field)
    points = field[0].shape[0] * pieces // (2 * fl)
    width = field[0].shape[1]
    ts = tile_of(width, FORWARD_TILE)
    group = FORWARD_GROUP if fl % FORWARD_GROUP == 0 else 1
    depth = min(FORWARD_DEPTH, width // ts * fl // group)
    body = functools.partial(forward_body, pieces=pieces, points=points, base=base, steps=width // ts)
    if init is None:
        inner, start = body, []
        body = lambda turn, k, al, *rest: inner(turn, k, al, None, *rest)
    else:
        start = [init]
    specs = [pl.BlockSpec(memory_space=pltpu.SMEM), pl.BlockSpec(memory_space=pl.ANY), in_vmem()]
    return pl.pallas_call(
        body,
        in_specs=specs + [in_vmem()] * (len(start) + pieces),
        out_specs=in_vmem(),
        out_shape=jax.ShapeDtypeStruct((2 * points * fl + 8, receivers), F32),
        scratch_shapes=[
            pltpu.VMEM((depth, 2, group, receivers, ts), BF16),
            pltpu.SemaphoreType.DMA((depth,)),
            pltpu.VMEM((ts // LANES, 2 * points * fl, LANES), F32),
            pltpu.VMEM((fl // group, 2 * points * group, 2 * receivers * group), F32),
        ],
        compiler_params=pltpu.CompilerParams(vmem_limit_bytes=VMEM_LIMIT),
        cost_estimate=pl.CostEstimate(
            flops=64 * points * receivers * width * fl, bytes_accessed=4 * fl * receivers * width, transcendentals=0
        ),
        name="forward",
    )(turn, kernel, alignment, *start, *field)


def split(whole):
    high = whole.astype(BF16)
    return high, (whole - high.astype(F32)).astype(BF16)


def taper_body(t_ref, *refs, inputs, points, rows):
    g_refs, d_refs, al_ref = refs[:inputs], refs[inputs:-1], refs[-1]
    width = g_refs[0].shape[1]
    step = min(512, width)
    own = len(d_refs) * rows
    total = jnp.zeros((8, LANES), F32)
    for p in range(points):
        high, low = split(t_ref[p])
        places = [
            (ref, slice(at, at + rows)) for ref in g_refs for at in range(p * rows, ref.shape[0], points * rows)
        ]
        for at in range(0, width, step):
            cols = slice(at, at + step)
            g = jnp.concatenate([ref[place, cols] for ref, place in places], 0)
            d = jnp.dot(low, g, preferred_element_type=F32)
            d += jnp.dot(high, g, preferred_element_type=F32)
            for k, ref in enumerate(d_refs):
                ref[p * rows : (p + 1) * rows, cols] = d[k * rows : (k + 1) * rows].astype(BF16)
            product = d * g[:own].astype(F32)
            for j in range(0, step, LANES):
                total += product[:, j : j + LANES].reshape(own // 8, 8, LANES).sum(0)
    al_ref[...] = total


def taper(matrices, blocks, outputs, rows):
    points = matrices.shape[0]
    width = blocks[0].shape[1]
    return pl.pallas_call(
        functools.partial(taper_body, inputs=len(blocks), points=points, rows=rows),
        in_specs=[in_vmem()] * (1 + len(blocks)),
        out_specs=[in_vmem()] * (outputs + 1),
        out_shape=[jax.ShapeDtypeStruct((points * rows, width), BF16)] * outputs
        + [jax.ShapeDtypeStruct((8, LANES), F32)],
        compiler_params=pltpu.CompilerParams(vmem_limit_bytes=VMEM_LIMIT),
        cost_estimate=pl.CostEstimate(
            flops=6 * matrices.size * width, bytes_accessed=8 * points * rows * outputs * width, transcendentals=0
        ),
        name="taper",
    )(matrices, *blocks)


def merge_body(own_ref, got_ref, p_ref, sums_ref):
    size, receivers = p_ref.shape
    projected = own_ref[:size] + got_ref[:size]
    p_ref[...] = projected
    squares = jnp.sum((projected * projected).reshape(size // 8, 8, receivers), 0)
    pad = -receivers % LANES
    if pad:
        squares = jnp.concatenate([squares, jnp.zeros((8, pad), F32)], 1)
    curvature = sum(squares[:, j : j + LANES] for j in range(0, receivers + pad, LANES))
    alignment = own_ref[size:, :LANES] + got_ref[size:, :LANES]
    for at in range(0, sums_ref.shape[0], 16):
        sums_ref[at : at + 8] = alignment
        sums_ref[at + 8 : at + 16] = curvature


def merge(own, got, count):
    size, receivers = own.shape
    return pl.pallas_call(
        merge_body,
        in_specs=[in_vmem()] * 2,
        out_specs=[in_vmem()] * 2,
        out_shape=[jax.ShapeDtypeStruct((size - 8, receivers), F32), jax.ShapeDtypeStruct((16 * count, LANES), F32)],
        name="merge",
    )(own, got)


def step_body(p_ref, r_ref, s_ref, a_ref, new_ref, l_ref, *, fl, points):
    receivers = p_ref.shape[1]
    sums = sum(s_ref[at : at + 16] for at in range(0, s_ref.shape[0], 16))
    length = jnp.sum(sums[0:8], keepdims=True) / jnp.sum(sums[8:16], keepdims=True)
    a_ref[...] = jnp.broadcast_to(length, a_ref.shape)
    new = r_ref[...] - length * p_ref[...]
    new_ref[...] = new
    for f in range(fl):
        block = new[2 * points * f : 2 * points * (f + 1)]
        real, imag = block[:points], block[points:]
        l_ref[f, :, :receivers] = block.astype(BF16)
        l_ref[f, :, receivers:] = jnp.concatenate([imag, -real], 0).astype(BF16)


def advance(projected, residual, sums, fl, points):
    receivers = projected.shape[1]
    return pl.pallas_call(
        functools.partial(step_body, fl=fl, points=points),
        in_specs=[in_vmem()] * 3,
        out_specs=[in_vmem()] * 3,
        out_shape=[
            jax.ShapeDtypeStruct((8, LANES), F32),
            jax.ShapeDtypeStruct(projected.shape, F32),
            jax.ShapeDtypeStruct((fl, 2 * points, 2 * receivers), BF16),
        ],
        name="step",
    )(projected, residual, sums)


def wave_table(freqs, fl):
    samples = np.arange(NT)[:, None]
    phase = (samples * np.arange(freqs)[None, :] % NT) * (2.0 * math.pi / NT)
    table = np.stack([np.cos(phase), -np.sin(phase)], 1) * freqs**-0.5
    table = table.reshape(NT, 2, freqs // fl, fl).transpose(0, 2, 1, 3)
    return table.reshape(NT, 2 * freqs).astype(np.float32)


def swap(x):
    return lax.ppermute(x, "src", [(0, 1), (1, 0)])


def estimate_body(*refs, spans, pieces, fl, points):
    turn_ref, lengths = refs[0], refs[1 : 1 + ITERS]
    fields, (e_ref, scr) = refs[1 + ITERS : -2], refs[-2:]
    lengths = [ref[0:1, 0:1] for ref in lengths]
    at = 0
    for part, ((base, width), count) in enumerate(zip(spans, pieces)):
        size = 2 * points * fl // count
        turn = turn_ref[part]

        def one(i, carry, at=at, base=base, count=count, size=size, turn=turn):
            off = pl.multiple_of(i * LANES, LANES)
            for k in range(count):
                value = sum(
                    lengths[n] * fields[at + n * count + k][:, pl.ds(off, LANES)].astype(F32) for n in range(ITERS)
                )
                scr[i % 2, pl.ds(pl.multiple_of((turn ^ k) * size, size), size), :] = value
            for c in range(2):
                for f in range(fl):
                    out = pl.ds(pl.multiple_of(base + i * LANES, LANES), LANES)
                    e_ref[c, f, :, out] = scr[i % 2, pl.ds(c * fl + f, points, stride=2 * fl), :]
            return carry

        lax.fori_loop(0, width // LANES, one, 0, unroll=2)
        at += ITERS * count


def estimate_of(turns, lengths, fields, spans, fl, points):
    parts = range(len(spans))
    flat = [x for part in parts for field in fields for x in field[part]]
    sources = sum(width for _, width in spans)
    return pl.pallas_call(
        functools.partial(
            estimate_body, spans=spans, pieces=[len(fields[0][part]) for part in parts], fl=fl, points=points
        ),
        in_specs=[pl.BlockSpec(memory_space=pltpu.SMEM)] + [in_vmem()] * (len(lengths) + len(flat)),
        out_specs=in_vmem(),
        out_shape=jax.ShapeDtypeStruct((2, fl, points, sources), F32),
        scratch_shapes=[pltpu.VMEM((2, 2 * points * fl, LANES), F32)],
        compiler_params=pltpu.CompilerParams(vmem_limit_bytes=VMEM_LIMIT),
        name="estimate",
    )(turns, *lengths, *flat)


def then(x, *earlier):
    return lax.optimization_barrier((x, *earlier))[0]


def send(x, hop):
    return lax.ppermute(x, "freq", [(i, i ^ hop) for i in range(lax.axis_size("freq"))])


def exchange(x, rows):
    width = x.shape[-1]
    return lax.all_to_all(x.reshape(-1, rows, width), "freq", 0, 0, tiled=True).reshape(-1, width)


def body(kernel, data, win_start, win_end):
    count = lax.axis_size("freq")
    src_count = lax.axis_size("src")
    _, fl, receivers, sources = kernel.shape
    points = data.shape[3]
    rows = 2 * fl
    me = lax.axis_index("freq")
    own = points // count
    permutes = count & (count - 1) == 0 and rows % 16 == 0 and own == 1
    inner = {"plain": 1, "direct": 1, "relay": 2}
    parts, base = [], 0
    for weight, mode in PARTS:
        width = sources * weight // sum(w for w, _ in PARTS)
        parts.append((base, width, mode if permutes else "plain"))
        base += width

    def turn_of(mode):
        turn = (me // inner[mode]).reshape(1).astype(jnp.int32)
        return jnp.zeros_like(turn) if mode == "plain" else turn

    def pieces_of(mode):
        return 1 if mode == "plain" else count // inner[mode]

    table = jnp.asarray(wave_table(fl * count, fl))
    samples = jnp.arange(NT, dtype=jnp.int32)[None, :]

    def matrices_of(mode):
        size = own * inner[mode]
        first = me // inner[mode] * size
        starts = lax.dynamic_slice_in_dim(win_start, first, size)[:, None]
        ends = lax.dynamic_slice_in_dim(win_end, first, size)[:, None]
        window = ((samples >= starts) & (samples < ends)).astype(F32)
        right = table
        if mode != "plain":
            blocks = table.reshape(NT, count, rows)
            order = [me ^ (k * inner[mode] + y) for y in range(inner[mode]) for k in range(pieces_of(mode))]
            right = jnp.concatenate([lax.dynamic_index_in_dim(blocks, b, 1, keepdims=False) for b in order], 1)
        left = right[:, : right.shape[1] // inner[mode]]
        return jnp.einsum("pta,tb->pab", window[:, :, None] * left, right, precision=lax.Precision.HIGHEST)

    matrices = {mode: matrices_of(mode) for mode in sorted({mode for _, _, mode in parts})}

    def scatter(blocks, mode):
        if mode == "plain":
            return [exchange(blocks[0], rows)]
        return [blocks[0]] + [send(blocks[k], k * inner[mode]) for k in range(1, len(blocks))]

    def pair_up(got, mode):
        if mode != "relay":
            return got
        if EARLY:
            rest = jnp.concatenate(got[1:], 0)
            return [got[0], rest, send(got[0], 1), send(rest, 1)]
        joined = jnp.concatenate(got, 0)
        return [joined, send(joined, 1)]

    def tapered(got, mode):
        if mode != "plain":
            *field, alignment = taper(matrices[mode], got, pieces_of(mode), rows)
            return field, alignment
        if own == 1:
            field, alignment = taper(matrices[mode], got, 1, count * rows)
            return [field], alignment
        width = got[0].shape[-1]
        got = got[0].reshape(count, own, rows, width)
        done = [
            taper(matrices[mode][p : p + 1], [got[:, p].reshape(-1, width)], 1, count * rows) for p in range(own)
        ]
        field = jnp.stack([d.reshape(count, rows, width) for d, _ in done], 1).reshape(-1, width)
        return [field], sum(a for _, a in done)

    residual = data.transpose(1, 0, 3, 2).reshape(2 * fl * points, receivers)
    real, imag = jnp.split(residual.reshape(fl, 2 * points, receivers).astype(BF16), 2, 1)
    lhs = jnp.concatenate([jnp.concatenate([real, imag], 1), jnp.concatenate([imag, -real], 1)], 2)
    lengths, fields = [], []
    for iteration in range(ITERS):
        image = None
        fields.append([])
        gradients, gathered, sent = [], [], []
        after = lhs
        for base, width, mode in parts:
            gradient = adjoint(turn_of(mode), kernel, after, base, width, pieces_of(mode))
            after = then(lhs, gradient[-1])
            gradients.append(gradient)
            if TIE and gathered and mode == "relay":
                gradient = [then(x, gathered[-1][TIE - 1]) for x in gradient]
            gathered.append(pair_up(scatter(gradient, mode), mode))
        for n, (_, _, mode) in enumerate(parts):
            got = gathered[n]
            if n + 1 < len(parts):
                got = [then(got[0], gradients[n + 1][-1])] + got[1:]
            field, alignment = tapered(got, mode)
            if TIE2 and sent and mode == "relay":
                field = [then(x, *sent[-1][1][1:]) for x in field]
            sent.append((field, scatter(field, mode), alignment))
        for n, (base, _, mode) in enumerate(parts):
            _, field, alignment = sent[n]
            if n + 1 < len(parts):
                field = [then(field[0], sent[n + 1][0][-1])] + field[1:]
            image = forward(turn_of(mode), kernel, field, alignment, image, base)
            fields[-1].append(field)
        got = swap(image) if src_count == 2 else lax.psum(image, "src") - image
        projected, sums = merge(image, got, count)
        length, residual, lhs = advance(projected, residual, exchange(sums, 16), fl, points)
        lengths.append(length)
    spans = [(base, width) for base, width, _ in parts]
    turns = jnp.concatenate([turn_of(mode) for _, _, mode in parts])
    estimate = estimate_of(turns, lengths, fields, spans, fl, points)
    share = receivers // src_count
    residual = residual.reshape(fl, 2, points, receivers)
    residual = lax.dynamic_slice_in_dim(residual, lax.axis_index("src") * share, share, 3)
    return estimate, residual.transpose(1, 0, 3, 2)


def solution(mesh):
    in_specs = (P("grp", "freq", None, "src"), P("grp", "freq", None, None), P("grp"), P("grp"))
    out_specs = (P("grp", "freq", None, "src"), P("grp", "freq", "src", None))
    return jax.shard_map(body, mesh=mesh, in_specs=in_specs, out_specs=out_specs, check_vma=False)
```

```python
import functools
import math

import jax
import jax.numpy as jnp
import numpy as np
from jax import lax
from jax.experimental import pallas as pl
from jax.experimental.pallas import tpu as pltpu
from jax.sharding import PartitionSpec as P

ITERS = 2
NT = 128
LANES = 128
BF16 = jnp.bfloat16
F32 = jnp.float32
VMEM_LIMIT = 32 * 2**20
PARTS = ((1, "relay"), (1, "relay"))
ADJOINT_TILE = 2048
ADJOINT_DEPTH = 9
FORWARD_TILE = 2048
FORWARD_DEPTH = 9
FORWARD_GROUP = 1


def in_vmem():
    return pl.BlockSpec(memory_space=pltpu.VMEM)


def tile_of(width, limit):
    return max(t for t in range(LANES, min(limit, width) + 1, LANES) if width % t == 0)


def stream(k_hbm, kbuf, sem, base, steps, step):
    depth, _, group, _, ts = kbuf.shape
    groups = k_hbm.shape[1] // group
    total = steps * groups

    def copy(i):
        off = pl.multiple_of(base + i // groups * ts, LANES)
        slot = i % depth
        source = k_hbm.at[:, pl.ds(i % groups * group, group), :, pl.ds(off, ts)]
        return pltpu.make_async_copy(source, kbuf.at[slot], sem.at[slot])

    for i in range(min(depth - 1, total)):
        copy(i).start()

    def body(i, carry):
        @pl.when(i + depth - 1 < total)
        def _():
            copy(i + depth - 1).start()

        copy(i).wait()
        step(i // groups, i % groups, kbuf.at[i % depth])
        return carry

    lax.fori_loop(0, total, body, 0)


def adjoint_body(turn_ref, l_ref, k_hbm, *refs, points, base, steps):
    *o_refs, kbuf, sem, scr = refs
    _, _, _, receivers, ts = kbuf.shape
    fl = k_hbm.shape[1]
    size = 2 * points * fl // len(o_refs)
    turn = turn_ref[0]

    def step(s, f, block):
        out = jnp.dot(l_ref[f], block[...].reshape(2 * receivers, ts), preferred_element_type=F32)
        for c in range(2):
            for j in range(ts // LANES):
                scr[j, pl.ds(c * fl + f, points, stride=2 * fl), :] = out[
                    c * points : (c + 1) * points, j * LANES : (j + 1) * LANES
                ]

        @pl.when(f == fl - 1)
        def _():
            for k, o_ref in enumerate(o_refs):
                rows = pl.ds(pl.multiple_of((turn ^ k) * size, size), size)
                for j in range(ts // LANES):
                    at = pl.ds(pl.multiple_of(s * ts + j * LANES, LANES), LANES)
                    o_ref[:, at] = scr[j, rows, :].astype(BF16)

    stream(k_hbm, kbuf, sem, base, steps, step)


def adjoint(turn, kernel, rows, base, width, pieces):
    _, fl, receivers, sources = kernel.shape
    points = rows.shape[1] // 2
    ts = tile_of(width, ADJOINT_TILE)
    depth = min(ADJOINT_DEPTH, width // ts * fl)
    return pl.pallas_call(
        functools.partial(adjoint_body, points=points, base=base, steps=width // ts),
        in_specs=[pl.BlockSpec(memory_space=pltpu.SMEM), in_vmem(), pl.BlockSpec(memory_space=pl.ANY)],
        out_specs=[in_vmem()] * pieces,
        out_shape=[jax.ShapeDtypeStruct((2 * points * fl // pieces, width), BF16)] * pieces,
        scratch_shapes=[
            pltpu.VMEM((depth, 2, 1, receivers, ts), BF16),
            pltpu.SemaphoreType.DMA((depth,)),
            pltpu.VMEM((ts // LANES, 2 * points * fl, LANES), F32),
        ],
        compiler_params=pltpu.CompilerParams(vmem_limit_bytes=VMEM_LIMIT),
        cost_estimate=pl.CostEstimate(
            flops=64 * points * receivers * width * fl, bytes_accessed=4 * fl * receivers * width, transcendentals=0
        ),
        name="adjoint",
    )(turn, rows, kernel)


def forward_body(turn_ref, k_hbm, al_ref, init_ref, *refs, pieces, points, base, steps):
    d_refs, (o_ref, kbuf, sem, dscr, acc) = refs[:pieces], refs[pieces:]
    _, _, group, receivers, ts = kbuf.shape
    fl = k_hbm.shape[1]
    size = 2 * points * fl // pieces
    turn = turn_ref[0]
    acc[...] = jnp.zeros(acc.shape, F32)

    def step(s, n, block):
        tiles = range(ts // LANES)

        @pl.when(n == 0)
        def _():
            for k, d_ref in enumerate(d_refs):
                rows = pl.ds(pl.multiple_of((turn ^ k) * size, size), size)
                for j in tiles:
                    at = pl.ds(pl.multiple_of(s * ts + j * LANES, LANES), LANES)
                    dscr[j, rows, :] = d_ref[:, at].astype(F32)

        def part(c, f):
            rows = pl.ds(c * fl + n * group + f, points, stride=2 * fl)
            return jnp.concatenate([dscr[j, rows, :] for j in tiles], 1)

        field = jnp.concatenate([part(c, f) for f in range(group) for c in range(2)], 0).astype(BF16)
        acc[n] += lax.dot_general(
            field,
            block[...].reshape(2 * group * receivers, ts),
            (((1,), (1,)), ((), ())),
            preferred_element_type=F32,
        )

    stream(k_hbm, kbuf, sem, base, steps, step)
    for f in range(fl):
        n, g = divmod(f, group)
        whole = acc[n, 2 * points * g : 2 * points * (g + 1)]
        by_real = whole[:, g * receivers : (g + 1) * receivers]
        by_imag = whole[:, (group + g) * receivers : (group + g + 1) * receivers]
        top = 2 * points * f
        mid = top + points
        end = top + 2 * points
        real = by_real[:points] - by_imag[points:]
        imag = by_real[points:] + by_imag[:points]
        if init_ref is not None:
            real += init_ref[top:mid]
            imag += init_ref[mid:end]
        o_ref[top:mid] = real
        o_ref[mid:end] = imag
    extra = jnp.concatenate([al_ref[...], jnp.zeros((8, receivers - LANES), F32)], 1)
    if init_ref is not None:
        extra += init_ref[2 * points * fl :]
    o_ref[2 * points * fl :] = extra


def forward(turn, kernel, field, alignment, init, base):
    _, fl, receivers, sources = kernel.shape
    pieces = len(field)
    points = field[0].shape[0] * pieces // (2 * fl)
    width = field[0].shape[1]
    ts = tile_of(width, FORWARD_TILE)
    group = FORWARD_GROUP if fl % FORWARD_GROUP == 0 else 1
    depth = min(FORWARD_DEPTH, width // ts * fl // group)
    body = functools.partial(forward_body, pieces=pieces, points=points, base=base, steps=width // ts)
    if init is None:
        inner, start = body, []
        body = lambda turn, k, al, *rest: inner(turn, k, al, None, *rest)
    else:
        start = [init]
    specs = [pl.BlockSpec(memory_space=pltpu.SMEM), pl.BlockSpec(memory_space=pl.ANY), in_vmem()]
    return pl.pallas_call(
        body,
        in_specs=specs + [in_vmem()] * (len(start) + pieces),
        out_specs=in_vmem(),
        out_shape=jax.ShapeDtypeStruct((2 * points * fl + 8, receivers), F32),
        scratch_shapes=[
            pltpu.VMEM((depth, 2, group, receivers, ts), BF16),
            pltpu.SemaphoreType.DMA((depth,)),
            pltpu.VMEM((ts // LANES, 2 * points * fl, LANES), F32),
            pltpu.VMEM((fl // group, 2 * points * group, 2 * receivers * group), F32),
        ],
        compiler_params=pltpu.CompilerParams(vmem_limit_bytes=VMEM_LIMIT),
        cost_estimate=pl.CostEstimate(
            flops=64 * points * receivers * width * fl, bytes_accessed=4 * fl * receivers * width, transcendentals=0
        ),
        name="forward",
    )(turn, kernel, alignment, *start, *field)


def split(whole):
    high = whole.astype(BF16)
    return high, (whole - high.astype(F32)).astype(BF16)


def taper_body(t_ref, *refs, inputs, points, rows):
    g_refs, d_refs, al_ref = refs[:inputs], refs[inputs:-1], refs[-1]
    width = g_refs[0].shape[1]
    step = min(512, width)
    own = len(d_refs) * rows
    total = jnp.zeros((8, LANES), F32)
    for p in range(points):
        high, low = split(t_ref[p])
        places = [
            (ref, slice(at, at + rows)) for ref in g_refs for at in range(p * rows, ref.shape[0], points * rows)
        ]
        for at in range(0, width, step):
            cols = slice(at, at + step)
            g = jnp.concatenate([ref[place, cols] for ref, place in places], 0)
            d = jnp.dot(low, g, preferred_element_type=F32)
            d += jnp.dot(high, g, preferred_element_type=F32)
            for k, ref in enumerate(d_refs):
                ref[p * rows : (p + 1) * rows, cols] = d[k * rows : (k + 1) * rows].astype(BF16)
            product = d * g[:own].astype(F32)
            for j in range(0, step, LANES):
                total += product[:, j : j + LANES].reshape(own // 8, 8, LANES).sum(0)
    al_ref[...] = total


def taper(matrices, blocks, outputs, rows):
    points = matrices.shape[0]
    width = blocks[0].shape[1]
    return pl.pallas_call(
        functools.partial(taper_body, inputs=len(blocks), points=points, rows=rows),
        in_specs=[in_vmem()] * (1 + len(blocks)),
        out_specs=[in_vmem()] * (outputs + 1),
        out_shape=[jax.ShapeDtypeStruct((points * rows, width), BF16)] * outputs
        + [jax.ShapeDtypeStruct((8, LANES), F32)],
        compiler_params=pltpu.CompilerParams(vmem_limit_bytes=VMEM_LIMIT),
        cost_estimate=pl.CostEstimate(
            flops=6 * matrices.size * width, bytes_accessed=8 * points * rows * outputs * width, transcendentals=0
        ),
        name="taper",
    )(matrices, *blocks)


def merge_body(own_ref, got_ref, p_ref, sums_ref):
    size, receivers = p_ref.shape
    projected = own_ref[:size] + got_ref[:size]
    p_ref[...] = projected
    squares = jnp.sum((projected * projected).reshape(size // 8, 8, receivers), 0)
    pad = -receivers % LANES
    if pad:
        squares = jnp.concatenate([squares, jnp.zeros((8, pad), F32)], 1)
    curvature = sum(squares[:, j : j + LANES] for j in range(0, receivers + pad, LANES))
    alignment = own_ref[size:, :LANES] + got_ref[size:, :LANES]
    for at in range(0, sums_ref.shape[0], 16):
        sums_ref[at : at + 8] = alignment
        sums_ref[at + 8 : at + 16] = curvature


def merge(own, got, count):
    size, receivers = own.shape
    return pl.pallas_call(
        merge_body,
        in_specs=[in_vmem()] * 2,
        out_specs=[in_vmem()] * 2,
        out_shape=[jax.ShapeDtypeStruct((size - 8, receivers), F32), jax.ShapeDtypeStruct((16 * count, LANES), F32)],
        name="merge",
    )(own, got)


def step_body(p_ref, r_ref, s_ref, a_ref, new_ref, l_ref, *, fl, points):
    receivers = p_ref.shape[1]
    length = step_length(s_ref)
    a_ref[...] = jnp.broadcast_to(length, a_ref.shape)
    new = r_ref[...] - length * p_ref[...]
    new_ref[...] = new
    for f in range(fl):
        block = new[2 * points * f : 2 * points * (f + 1)]
        real, imag = block[:points], block[points:]
        l_ref[f, :, :receivers] = block.astype(BF16)
        l_ref[f, :, receivers:] = jnp.concatenate([imag, -real], 0).astype(BF16)


def advance(projected, residual, sums, fl, points):
    receivers = projected.shape[1]
    return pl.pallas_call(
        functools.partial(step_body, fl=fl, points=points),
        in_specs=[in_vmem()] * 3,
        out_specs=[in_vmem()] * 3,
        out_shape=[
            jax.ShapeDtypeStruct((8, LANES), F32),
            jax.ShapeDtypeStruct(projected.shape, F32),
            jax.ShapeDtypeStruct((fl, 2 * points, 2 * receivers), BF16),
        ],
        name="step",
    )(projected, residual, sums)


def wave_table(freqs, fl):
    samples = np.arange(NT)[:, None]
    phase = (samples * np.arange(freqs)[None, :] % NT) * (2.0 * math.pi / NT)
    table = np.stack([np.cos(phase), -np.sin(phase)], 1) * freqs**-0.5
    table = table.reshape(NT, 2, freqs // fl, fl).transpose(0, 2, 1, 3)
    return table.reshape(NT, 2 * freqs).astype(np.float32)


def swap(x):
    return lax.ppermute(x, "src", [(0, 1), (1, 0)])


def step_length(s_ref):
    sums = sum(s_ref[at : at + 16] for at in range(0, s_ref.shape[0], 16))
    return jnp.sum(sums[0:8], keepdims=True) / jnp.sum(sums[8:16], keepdims=True)


def finish_body(place_ref, s_ref, p_ref, r_ref, *refs, spans, pieces):
    earlier, fields, (e_hbm, out_ref, stage, scr, sem) = refs[: ITERS - 1], refs[ITERS - 1 : -5], refs[-5:]
    _, fl, points, share = out_ref.shape
    lengths = [ref[0:1, 0:1] for ref in earlier] + [step_length(s_ref)]
    copies = []
    at = 0
    for part, ((base, width), count) in enumerate(zip(spans, pieces)):
        size = 2 * points * fl // count
        turn = place_ref[1 + part]

        def one(i, carry, at=at, base=base, count=count, size=size, turn=turn):
            off = pl.multiple_of(i * LANES, LANES)
            out = pl.ds(pl.multiple_of(base + i * LANES, LANES), LANES)
            for k in range(count):
                values = [fields[at + n * count + k][:, pl.ds(off, LANES)].astype(F32) for n in range(ITERS)]
                rows = pl.ds(pl.multiple_of((turn ^ k) * size, size), size)
                scr[i % 2, rows, :] = sum(a * x for a, x in zip(lengths, values))
            for c in range(2):
                for f in range(fl):
                    stage[c, f, :, out] = scr[i % 2, pl.ds(c * fl + f, points, stride=2 * fl), :]
            return carry

        lax.fori_loop(0, width // LANES, one, 0, unroll=2)
        span = pl.ds(base, width)
        copies.append(
            pltpu.make_async_copy(stage.at[:, :, :, span], e_hbm.at[:, :, :, span], sem.at[part])
        )
        copies[-1].start()
        at += ITERS * count
    residual = r_ref[...] - lengths[-1] * p_ref[...]
    mine = residual[:, :share]
    for n in range(1, residual.shape[1] // share):
        mine = jnp.where(place_ref[0] == n, residual[:, n * share : (n + 1) * share], mine)
    for c in range(2):
        for f in range(fl):
            top = (2 * f + c) * points
            out_ref[c, f] = mine[top : top + points]
    for copy in copies:
        copy.wait()


def finish(core, turns, sums, projected, residual, lengths, fields, spans, fl, points, share):
    parts = range(len(spans))
    flat = [x for part in parts for field in fields for x in field[part]]
    shape = (2, fl, points, sum(width for _, width in spans))
    return pl.pallas_call(
        functools.partial(finish_body, spans=spans, pieces=[len(fields[0][part]) for part in parts]),
        in_specs=[pl.BlockSpec(memory_space=pltpu.SMEM)] + [in_vmem()] * (3 + len(lengths) + len(flat)),
        out_specs=[pl.BlockSpec(memory_space=pl.ANY), in_vmem()],
        out_shape=[jax.ShapeDtypeStruct(shape, F32), jax.ShapeDtypeStruct((2, fl, points, share), F32)],
        scratch_shapes=[
            pltpu.VMEM(shape, F32),
            pltpu.VMEM((2, 2 * points * fl, LANES), F32),
            pltpu.SemaphoreType.DMA((len(spans),)),
        ],
        compiler_params=pltpu.CompilerParams(vmem_limit_bytes=VMEM_LIMIT),
        name="finish",
    )(jnp.concatenate([core] + turns), sums, projected, residual, *lengths, *flat)


def then(x, *earlier):
    return lax.optimization_barrier((x, *earlier))[0]


def send(x, hop):
    return lax.ppermute(x, "freq", [(i, i ^ hop) for i in range(lax.axis_size("freq"))])


def exchange(x, rows):
    width = x.shape[-1]
    return lax.all_to_all(x.reshape(-1, rows, width), "freq", 0, 0, tiled=True).reshape(-1, width)


def body(kernel, data, win_start, win_end):
    count = lax.axis_size("freq")
    src_count = lax.axis_size("src")
    _, fl, receivers, sources = kernel.shape
    points = data.shape[3]
    rows = 2 * fl
    me = lax.axis_index("freq")
    own = points // count
    permutes = count & (count - 1) == 0 and rows % 16 == 0 and own == 1
    inner = {"plain": 1, "direct": 1, "relay": 2}
    parts, base = [], 0
    for weight, mode in PARTS:
        width = sources * weight // sum(w for w, _ in PARTS)
        parts.append((base, width, mode if permutes else "plain"))
        base += width

    def turn_of(mode):
        turn = (me // inner[mode]).reshape(1).astype(jnp.int32)
        return jnp.zeros_like(turn) if mode == "plain" else turn

    def pieces_of(mode):
        return 1 if mode == "plain" else count // inner[mode]

    table = jnp.asarray(wave_table(fl * count, fl))
    samples = jnp.arange(NT, dtype=jnp.int32)[None, :]

    def matrices_of(mode):
        size = own * inner[mode]
        first = me // inner[mode] * size
        starts = lax.dynamic_slice_in_dim(win_start, first, size)[:, None]
        ends = lax.dynamic_slice_in_dim(win_end, first, size)[:, None]
        window = ((samples >= starts) & (samples < ends)).astype(F32)
        right = table
        if mode != "plain":
            blocks = table.reshape(NT, count, rows)
            order = [me ^ (k * inner[mode] + y) for y in range(inner[mode]) for k in range(pieces_of(mode))]
            right = jnp.concatenate([lax.dynamic_index_in_dim(blocks, b, 1, keepdims=False) for b in order], 1)
        left = right[:, : right.shape[1] // inner[mode]]
        return jnp.einsum("pta,tb->pab", window[:, :, None] * left, right, precision=lax.Precision.HIGHEST)

    matrices = {mode: matrices_of(mode) for mode in sorted({mode for _, _, mode in parts})}

    def scatter(blocks, mode):
        if mode == "plain":
            return [exchange(blocks[0], rows)]
        return [blocks[0]] + [send(blocks[k], k * inner[mode]) for k in range(1, len(blocks))]

    def pair_up(got, mode):
        if mode != "relay":
            return got
        joined = jnp.concatenate(got, 0)
        return [joined, send(joined, 1)]

    def tapered(got, mode):
        if mode != "plain":
            *field, alignment = taper(matrices[mode], got, pieces_of(mode), rows)
            return field, alignment
        if own == 1:
            field, alignment = taper(matrices[mode], got, 1, count * rows)
            return [field], alignment
        width = got[0].shape[-1]
        got = got[0].reshape(count, own, rows, width)
        done = [
            taper(matrices[mode][p : p + 1], [got[:, p].reshape(-1, width)], 1, count * rows) for p in range(own)
        ]
        field = jnp.stack([d.reshape(count, rows, width) for d, _ in done], 1).reshape(-1, width)
        return [field], sum(a for _, a in done)

    residual = data.transpose(1, 0, 3, 2).reshape(2 * fl * points, receivers)
    real, imag = jnp.split(residual.reshape(fl, 2 * points, receivers).astype(BF16), 2, 1)
    lhs = jnp.concatenate([jnp.concatenate([real, imag], 1), jnp.concatenate([imag, -real], 1)], 2)
    lengths, fields = [], []
    for iteration in range(ITERS):
        image = None
        fields.append([])
        gradients, gathered, sent = [], [], []
        after = lhs
        for base, width, mode in parts:
            gradient = adjoint(turn_of(mode), kernel, after, base, width, pieces_of(mode))
            after = then(lhs, gradient[-1])
            gradients.append(gradient)
            if gathered and mode == "relay":
                gradient = [then(x, gathered[-1][0]) for x in gradient]
            gathered.append(pair_up(scatter(gradient, mode), mode))
        for n, (_, _, mode) in enumerate(parts):
            got = gathered[n]
            if n + 1 < len(parts):
                got = [then(got[0], gradients[n + 1][-1])] + got[1:]
            field, alignment = tapered(got, mode)
            if sent and mode == "relay":
                field = [then(x, *sent[-1][1][1:]) for x in field]
            sent.append((field, scatter(field, mode), alignment))
        for n, (base, _, mode) in enumerate(parts):
            _, field, alignment = sent[n]
            if n + 1 < len(parts):
                field = [then(field[0], sent[n + 1][0][-1])] + field[1:]
            image = forward(turn_of(mode), kernel, field, alignment, image, base)
            fields[-1].append(field)
        got = swap(image) if src_count == 2 else lax.psum(image, "src") - image
        projected, sums = merge(image, got, count)
        sums = exchange(sums, 16)
        if iteration + 1 < ITERS:
            length, residual, lhs = advance(projected, residual, sums, fl, points)
            lengths.append(length)
    spans = [(base, width) for base, width, _ in parts]
    turns = [turn_of(mode) for _, _, mode in parts]
    core = lax.axis_index("src").reshape(1).astype(jnp.int32)
    share = receivers // src_count
    estimate, residual = finish(
        core, turns, sums, projected, residual, lengths, fields, spans, fl, points, share
    )
    return estimate, residual.transpose(0, 1, 3, 2)


def solution(mesh):
    in_specs = (P("grp", "freq", None, "src"), P("grp", "freq", None, None), P("grp"), P("grp"))
    out_specs = (P("grp", "freq", None, "src"), P("grp", "freq", "src", None))
    return jax.shard_map(body, mesh=mesh, in_specs=in_specs, out_specs=out_specs, check_vma=False)
```

```python
import functools
import math

import jax
import jax.numpy as jnp
import numpy as np
from jax import lax
from jax.experimental import pallas as pl
from jax.experimental.pallas import tpu as pltpu
from jax.sharding import PartitionSpec as P

ITERS = 2
NT = 128
LANES = 128
BF16 = jnp.bfloat16
F32 = jnp.float32
VMEM_LIMIT = 32 * 2**20
PARTS = ((1, "relay"), (1, "relay"))
ADJOINT_TILE = 2048
ADJOINT_DEPTH = 9
FORWARD_TILE = 2048
FORWARD_DEPTH = 9
FORWARD_GROUP = 1


def in_vmem():
    return pl.BlockSpec(memory_space=pltpu.VMEM)


def tile_of(width, limit):
    return max(t for t in range(LANES, min(limit, width) + 1, LANES) if width % t == 0)


def stream(k_hbm, kbuf, sem, base, steps, step, first=lambda: None):
    depth, _, group, _, ts = kbuf.shape
    groups = k_hbm.shape[1] // group
    total = steps * groups

    def copy(i):
        off = pl.multiple_of(base + i // groups * ts, LANES)
        slot = i % depth
        source = k_hbm.at[:, pl.ds(i % groups * group, group), :, pl.ds(off, ts)]
        return pltpu.make_async_copy(source, kbuf.at[slot], sem.at[slot])

    for i in range(min(depth - 1, total)):
        copy(i).start()
    first()

    def body(i, carry):
        @pl.when(i + depth - 1 < total)
        def _():
            copy(i + depth - 1).start()

        copy(i).wait()
        step(i // groups, i % groups, kbuf.at[i % depth])
        return carry

    lax.fori_loop(0, total, body, 0)


def adjoint_body(turn_ref, k_hbm, *refs, pieces, points, base, steps, stage):
    ins, refs = refs[: STAGES[stage]], refs[STAGES[stage] :]
    o_refs, refs = refs[:pieces], refs[pieces:]
    made, (kbuf, sem, scr) = refs[:-3], refs[-3:]
    _, _, _, receivers, ts = kbuf.shape
    fl = k_hbm.shape[1]
    size = 2 * points * fl // pieces
    turn = turn_ref[0]
    l_ref = made[0] if made else ins[0]

    def first():
        if stage == "rest":
            return
        if stage == "step":
            length = step_length(ins[1])
            made[2][...] = jnp.broadcast_to(length, made[2].shape)
        for f in range(fl):
            real, imag = ins[0][0, f], ins[0][1, f]
            if stage == "step":
                top = 2 * points * f
                real = real - length * ins[2][top : top + points]
                imag = imag - length * ins[2][top + points : top + 2 * points]
                made[1][0, f] = real
                made[1][1, f] = imag
            l_ref[f, :, :receivers] = jnp.concatenate([real, imag], 0).astype(BF16)
            l_ref[f, :, receivers:] = jnp.concatenate([imag, -real], 0).astype(BF16)

    def step(s, f, block):
        out = jnp.dot(l_ref[f], block[...].reshape(2 * receivers, ts), preferred_element_type=F32)
        for c in range(2):
            for j in range(ts // LANES):
                scr[j, pl.ds(c * fl + f, points, stride=2 * fl), :] = out[
                    c * points : (c + 1) * points, j * LANES : (j + 1) * LANES
                ]

        @pl.when(f == fl - 1)
        def _():
            for k, o_ref in enumerate(o_refs):
                rows = pl.ds(pl.multiple_of((turn ^ k) * size, size), size)
                for j in range(ts // LANES):
                    at = pl.ds(pl.multiple_of(s * ts + j * LANES, LANES), LANES)
                    o_ref[:, at] = scr[j, rows, :].astype(BF16)

    stream(k_hbm, kbuf, sem, base, steps, step, first)


STAGES = {"data": 1, "step": 3, "rest": 1}


def adjoint(turn, kernel, ins, stage, points, base, width, pieces):
    _, fl, receivers, sources = kernel.shape
    ts = tile_of(width, ADJOINT_TILE)
    depth = min(ADJOINT_DEPTH, width // ts * fl)
    shapes = [jax.ShapeDtypeStruct((2 * points * fl // pieces, width), BF16)] * pieces
    if stage != "rest":
        shapes.append(jax.ShapeDtypeStruct((fl, 2 * points, 2 * receivers), BF16))
    if stage == "step":
        shapes.append(jax.ShapeDtypeStruct((2, fl, points, receivers), F32))
        shapes.append(jax.ShapeDtypeStruct((8, LANES), F32))
    out = pl.pallas_call(
        functools.partial(
            adjoint_body, pieces=pieces, points=points, base=base, steps=width // ts, stage=stage
        ),
        in_specs=[pl.BlockSpec(memory_space=pltpu.SMEM), pl.BlockSpec(memory_space=pl.ANY)] + [in_vmem()] * len(ins),
        out_specs=[in_vmem()] * len(shapes),
        out_shape=shapes,
        scratch_shapes=[
            pltpu.VMEM((depth, 2, 1, receivers, ts), BF16),
            pltpu.SemaphoreType.DMA((depth,)),
            pltpu.VMEM((ts // LANES, 2 * points * fl, LANES), F32),
        ],
        compiler_params=pltpu.CompilerParams(vmem_limit_bytes=VMEM_LIMIT),
        cost_estimate=pl.CostEstimate(
            flops=64 * points * receivers * width * fl, bytes_accessed=4 * fl * receivers * width, transcendentals=0
        ),
        name="adjoint",
    )(turn, kernel, *ins)
    return out[:pieces], out[pieces:]


def forward_body(turn_ref, k_hbm, al_ref, init_ref, *refs, pieces, points, base, steps):
    d_refs, (o_ref, kbuf, sem, dscr, acc) = refs[:pieces], refs[pieces:]
    _, _, group, receivers, ts = kbuf.shape
    fl = k_hbm.shape[1]
    size = 2 * points * fl // pieces
    turn = turn_ref[0]
    acc[...] = jnp.zeros(acc.shape, F32)

    def step(s, n, block):
        tiles = range(ts // LANES)

        @pl.when(n == 0)
        def _():
            for k, d_ref in enumerate(d_refs):
                rows = pl.ds(pl.multiple_of((turn ^ k) * size, size), size)
                for j in tiles:
                    at = pl.ds(pl.multiple_of(s * ts + j * LANES, LANES), LANES)
                    dscr[j, rows, :] = d_ref[:, at].astype(F32)

        def part(c, f):
            rows = pl.ds(c * fl + n * group + f, points, stride=2 * fl)
            return jnp.concatenate([dscr[j, rows, :] for j in tiles], 1)

        field = jnp.concatenate([part(c, f) for f in range(group) for c in range(2)], 0).astype(BF16)
        acc[n] += lax.dot_general(
            field,
            block[...].reshape(2 * group * receivers, ts),
            (((1,), (1,)), ((), ())),
            preferred_element_type=F32,
        )

    stream(k_hbm, kbuf, sem, base, steps, step)
    for f in range(fl):
        n, g = divmod(f, group)
        whole = acc[n, 2 * points * g : 2 * points * (g + 1)]
        by_real = whole[:, g * receivers : (g + 1) * receivers]
        by_imag = whole[:, (group + g) * receivers : (group + g + 1) * receivers]
        top = 2 * points * f
        mid = top + points
        end = top + 2 * points
        real = by_real[:points] - by_imag[points:]
        imag = by_real[points:] + by_imag[:points]
        if init_ref is not None:
            real += init_ref[top:mid]
            imag += init_ref[mid:end]
        o_ref[top:mid] = real
        o_ref[mid:end] = imag
    extra = jnp.concatenate([al_ref[...], jnp.zeros((8, receivers - LANES), F32)], 1)
    if init_ref is not None:
        extra += init_ref[2 * points * fl :]
    o_ref[2 * points * fl :] = extra


def forward(turn, kernel, field, alignment, init, base):
    _, fl, receivers, sources = kernel.shape
    pieces = len(field)
    points = field[0].shape[0] * pieces // (2 * fl)
    width = field[0].shape[1]
    ts = tile_of(width, FORWARD_TILE)
    group = FORWARD_GROUP if fl % FORWARD_GROUP == 0 else 1
    depth = min(FORWARD_DEPTH, width // ts * fl // group)
    body = functools.partial(forward_body, pieces=pieces, points=points, base=base, steps=width // ts)
    if init is None:
        inner, start = body, []
        body = lambda turn, k, al, *rest: inner(turn, k, al, None, *rest)
    else:
        start = [init]
    specs = [pl.BlockSpec(memory_space=pltpu.SMEM), pl.BlockSpec(memory_space=pl.ANY), in_vmem()]
    return pl.pallas_call(
        body,
        in_specs=specs + [in_vmem()] * (len(start) + pieces),
        out_specs=in_vmem(),
        out_shape=jax.ShapeDtypeStruct((2 * points * fl + 8, receivers), F32),
        scratch_shapes=[
            pltpu.VMEM((depth, 2, group, receivers, ts), BF16),
            pltpu.SemaphoreType.DMA((depth,)),
            pltpu.VMEM((ts // LANES, 2 * points * fl, LANES), F32),
            pltpu.VMEM((fl // group, 2 * points * group, 2 * receivers * group), F32),
        ],
        compiler_params=pltpu.CompilerParams(vmem_limit_bytes=VMEM_LIMIT),
        cost_estimate=pl.CostEstimate(
            flops=64 * points * receivers * width * fl, bytes_accessed=4 * fl * receivers * width, transcendentals=0
        ),
        name="forward",
    )(turn, kernel, alignment, *start, *field)


def split(whole):
    high = whole.astype(BF16)
    return high, (whole - high.astype(F32)).astype(BF16)


def taper_body(t_ref, *refs, inputs, points, rows):
    g_refs, d_refs, al_ref = refs[:inputs], refs[inputs:-1], refs[-1]
    width = g_refs[0].shape[1]
    step = min(512, width)
    own = len(d_refs) * rows
    total = jnp.zeros((8, LANES), F32)
    for p in range(points):
        high, low = split(t_ref[p])
        places = [
            (ref, slice(at, at + rows)) for ref in g_refs for at in range(p * rows, ref.shape[0], points * rows)
        ]
        for at in range(0, width, step):
            cols = slice(at, at + step)
            g = jnp.concatenate([ref[place, cols] for ref, place in places], 0)
            d = jnp.dot(low, g, preferred_element_type=F32)
            d += jnp.dot(high, g, preferred_element_type=F32)
            for k, ref in enumerate(d_refs):
                ref[p * rows : (p + 1) * rows, cols] = d[k * rows : (k + 1) * rows].astype(BF16)
            product = d * g[:own].astype(F32)
            for j in range(0, step, LANES):
                total += product[:, j : j + LANES].reshape(own // 8, 8, LANES).sum(0)
    al_ref[...] = total


def taper(matrices, blocks, outputs, rows):
    points = matrices.shape[0]
    width = blocks[0].shape[1]
    return pl.pallas_call(
        functools.partial(taper_body, inputs=len(blocks), points=points, rows=rows),
        in_specs=[in_vmem()] * (1 + len(blocks)),
        out_specs=[in_vmem()] * (outputs + 1),
        out_shape=[jax.ShapeDtypeStruct((points * rows, width), BF16)] * outputs
        + [jax.ShapeDtypeStruct((8, LANES), F32)],
        compiler_params=pltpu.CompilerParams(vmem_limit_bytes=VMEM_LIMIT),
        cost_estimate=pl.CostEstimate(
            flops=6 * matrices.size * width, bytes_accessed=8 * points * rows * outputs * width, transcendentals=0
        ),
        name="taper",
    )(matrices, *blocks)


def merge_body(own_ref, got_ref, p_ref, sums_ref):
    size, receivers = p_ref.shape
    projected = own_ref[:size] + got_ref[:size]
    p_ref[...] = projected
    squares = jnp.sum((projected * projected).reshape(size // 8, 8, receivers), 0)
    pad = -receivers % LANES
    if pad:
        squares = jnp.concatenate([squares, jnp.zeros((8, pad), F32)], 1)
    curvature = sum(squares[:, j : j + LANES] for j in range(0, receivers + pad, LANES))
    alignment = own_ref[size:, :LANES] + got_ref[size:, :LANES]
    for at in range(0, sums_ref.shape[0], 16):
        sums_ref[at : at + 8] = alignment
        sums_ref[at + 8 : at + 16] = curvature


def merge(own, got, count):
    size, receivers = own.shape
    return pl.pallas_call(
        merge_body,
        in_specs=[in_vmem()] * 2,
        out_specs=[in_vmem()] * 2,
        out_shape=[jax.ShapeDtypeStruct((size - 8, receivers), F32), jax.ShapeDtypeStruct((16 * count, LANES), F32)],
        name="merge",
    )(own, got)


def wave_table(freqs, fl):
    samples = np.arange(NT)[:, None]
    phase = (samples * np.arange(freqs)[None, :] % NT) * (2.0 * math.pi / NT)
    table = np.stack([np.cos(phase), -np.sin(phase)], 1) * freqs**-0.5
    table = table.reshape(NT, 2, freqs // fl, fl).transpose(0, 2, 1, 3)
    return table.reshape(NT, 2 * freqs).astype(np.float32)


def swap(x):
    return lax.ppermute(x, "src", [(0, 1), (1, 0)])


def step_length(s_ref):
    sums = sum(s_ref[at : at + 16] for at in range(0, s_ref.shape[0], 16))
    return jnp.sum(sums[0:8], keepdims=True) / jnp.sum(sums[8:16], keepdims=True)


def finish_body(place_ref, s_ref, p_ref, r_ref, *refs, spans, pieces):
    earlier, fields, (e_hbm, out_ref, stage, scr, sem) = refs[: ITERS - 1], refs[ITERS - 1 : -5], refs[-5:]
    _, fl, points, share = out_ref.shape
    lengths = [ref[0:1, 0:1] for ref in earlier] + [step_length(s_ref)]
    copies = []
    at = 0
    for part, ((base, width), count) in enumerate(zip(spans, pieces)):
        size = 2 * points * fl // count
        turn = place_ref[1 + part]

        def one(i, carry, at=at, base=base, count=count, size=size, turn=turn):
            off = pl.multiple_of(i * LANES, LANES)
            out = pl.ds(pl.multiple_of(base + i * LANES, LANES), LANES)
            for k in range(count):
                values = [fields[at + n * count + k][:, pl.ds(off, LANES)].astype(F32) for n in range(ITERS)]
                rows = pl.ds(pl.multiple_of((turn ^ k) * size, size), size)
                scr[i % 2, rows, :] = sum(a * x for a, x in zip(lengths, values))
            for c in range(2):
                for f in range(fl):
                    stage[c, f, :, out] = scr[i % 2, pl.ds(c * fl + f, points, stride=2 * fl), :]
            return carry

        lax.fori_loop(0, width // LANES, one, 0, unroll=2)
        span = pl.ds(base, width)
        copies.append(
            pltpu.make_async_copy(stage.at[:, :, :, span], e_hbm.at[:, :, :, span], sem.at[part])
        )
        copies[-1].start()
        at += ITERS * count
    for c in range(2):
        for f in range(fl):
            top = (2 * f + c) * points
            residual = r_ref[c, f] - lengths[-1] * p_ref[top : top + points]
            mine = residual[:, :share]
            for n in range(1, residual.shape[1] // share):
                mine = jnp.where(place_ref[0] == n, residual[:, n * share : (n + 1) * share], mine)
            out_ref[c, f] = mine
    for copy in copies:
        copy.wait()


def finish(core, turns, sums, projected, residual, lengths, fields, spans, fl, points, share):
    parts = range(len(spans))
    flat = [x for part in parts for field in fields for x in field[part]]
    shape = (2, fl, points, sum(width for _, width in spans))
    return pl.pallas_call(
        functools.partial(finish_body, spans=spans, pieces=[len(fields[0][part]) for part in parts]),
        in_specs=[pl.BlockSpec(memory_space=pltpu.SMEM)] + [in_vmem()] * (3 + len(lengths) + len(flat)),
        out_specs=[pl.BlockSpec(memory_space=pl.ANY), in_vmem()],
        out_shape=[jax.ShapeDtypeStruct(shape, F32), jax.ShapeDtypeStruct((2, fl, points, share), F32)],
        scratch_shapes=[
            pltpu.VMEM(shape, F32),
            pltpu.VMEM((2, 2 * points * fl, LANES), F32),
            pltpu.SemaphoreType.DMA((len(spans),)),
        ],
        compiler_params=pltpu.CompilerParams(vmem_limit_bytes=VMEM_LIMIT),
        name="finish",
    )(jnp.concatenate([core] + turns), sums, projected, residual, *lengths, *flat)


def then(x, *earlier):
    return lax.optimization_barrier((x, *earlier))[0]


def send(x, hop):
    return lax.ppermute(x, "freq", [(i, i ^ hop) for i in range(lax.axis_size("freq"))])


def exchange(x, rows):
    width = x.shape[-1]
    return lax.all_to_all(x.reshape(-1, rows, width), "freq", 0, 0, tiled=True).reshape(-1, width)


def body(kernel, data, win_start, win_end):
    count = lax.axis_size("freq")
    src_count = lax.axis_size("src")
    _, fl, receivers, sources = kernel.shape
    points = data.shape[3]
    rows = 2 * fl
    me = lax.axis_index("freq")
    own = points // count
    permutes = count & (count - 1) == 0 and rows % 16 == 0 and own == 1
    inner = {"plain": 1, "direct": 1, "relay": 2}
    parts, base = [], 0
    for weight, mode in PARTS:
        width = sources * weight // sum(w for w, _ in PARTS)
        parts.append((base, width, mode if permutes else "plain"))
        base += width

    def turn_of(mode):
        turn = (me // inner[mode]).reshape(1).astype(jnp.int32)
        return jnp.zeros_like(turn) if mode == "plain" else turn

    def pieces_of(mode):
        return 1 if mode == "plain" else count // inner[mode]

    table = jnp.asarray(wave_table(fl * count, fl))
    samples = jnp.arange(NT, dtype=jnp.int32)[None, :]

    def matrices_of(mode):
        size = own * inner[mode]
        first = me // inner[mode] * size
        starts = lax.dynamic_slice_in_dim(win_start, first, size)[:, None]
        ends = lax.dynamic_slice_in_dim(win_end, first, size)[:, None]
        window = ((samples >= starts) & (samples < ends)).astype(F32)
        right = table
        if mode != "plain":
            blocks = table.reshape(NT, count, rows)
            order = [me ^ (k * inner[mode] + y) for y in range(inner[mode]) for k in range(pieces_of(mode))]
            right = jnp.concatenate([lax.dynamic_index_in_dim(blocks, b, 1, keepdims=False) for b in order], 1)
        left = right[:, : right.shape[1] // inner[mode]]
        return jnp.einsum("pta,tb->pab", window[:, :, None] * left, right, precision=lax.Precision.HIGHEST)

    matrices = {mode: matrices_of(mode) for mode in sorted({mode for _, _, mode in parts})}

    def scatter(blocks, mode):
        if mode == "plain":
            return [exchange(blocks[0], rows)]
        return [blocks[0]] + [send(blocks[k], k * inner[mode]) for k in range(1, len(blocks))]

    def pair_up(got, mode):
        if mode != "relay":
            return got
        joined = jnp.concatenate(got, 0)
        return [joined, send(joined, 1)]

    def tapered(got, mode):
        if mode != "plain":
            *field, alignment = taper(matrices[mode], got, pieces_of(mode), rows)
            return field, alignment
        if own == 1:
            field, alignment = taper(matrices[mode], got, 1, count * rows)
            return [field], alignment
        width = got[0].shape[-1]
        got = got[0].reshape(count, own, rows, width)
        done = [
            taper(matrices[mode][p : p + 1], [got[:, p].reshape(-1, width)], 1, count * rows) for p in range(own)
        ]
        field = jnp.stack([d.reshape(count, rows, width) for d, _ in done], 1).reshape(-1, width)
        return [field], sum(a for _, a in done)

    residual = data.transpose(0, 1, 3, 2)
    lengths, fields = [], []
    for iteration in range(ITERS):
        image = None
        fields.append([])
        gradients, gathered, sent = [], [], []
        if iteration == 0:
            stage, ins = "data", [residual]
        else:
            stage, ins = "step", [residual, sums, projected]
        for base, width, mode in parts:
            gradient, made = adjoint(turn_of(mode), kernel, ins, stage, points, base, width, pieces_of(mode))
            if stage == "step":
                residual = made[1]
                lengths.append(made[2])
            if made:
                lhs = made[0]
            stage, ins = "rest", [then(lhs, gradient[-1])]
            gradients.append(gradient)
            if gathered and mode == "relay":
                gradient = [then(x, gathered[-1][0]) for x in gradient]
            gathered.append(pair_up(scatter(gradient, mode), mode))
        for n, (_, _, mode) in enumerate(parts):
            got = gathered[n]
            if n + 1 < len(parts):
                got = [then(got[0], gradients[n + 1][-1])] + got[1:]
            field, alignment = tapered(got, mode)
            if sent and mode == "relay":
                field = [then(x, sent[-1][1][len(field) // 2]) for x in field]
            sent.append((field, scatter(field, mode), alignment))
        for n, (base, _, mode) in enumerate(parts):
            _, field, alignment = sent[n]
            if n + 1 < len(parts):
                field = [then(field[0], sent[n + 1][0][-1])] + field[1:]
            image = forward(turn_of(mode), kernel, field, alignment, image, base)
            fields[-1].append(field)
        got = swap(image) if src_count == 2 else lax.psum(image, "src") - image
        projected, sums = merge(image, got, count)
        sums = exchange(sums, 16)
    spans = [(base, width) for base, width, _ in parts]
    turns = [turn_of(mode) for _, _, mode in parts]
    core = lax.axis_index("src").reshape(1).astype(jnp.int32)
    share = receivers // src_count
    estimate, residual = finish(
        core, turns, sums, projected, residual, lengths, fields, spans, fl, points, share
    )
    return estimate, residual.transpose(0, 1, 3, 2)


def solution(mesh):
    in_specs = (P("grp", "freq", None, "src"), P("grp", "freq", None, None), P("grp"), P("grp"))
    out_specs = (P("grp", "freq", None, "src"), P("grp", "freq", "src", None))
    return jax.shard_map(body, mesh=mesh, in_specs=in_specs, out_specs=out_specs, check_vma=False)
```

```python
import functools
import math

import jax
import jax.numpy as jnp
import numpy as np
from jax import lax
from jax.experimental import pallas as pl
from jax.experimental.pallas import tpu as pltpu
from jax.sharding import PartitionSpec as P

ITERS = 2
NT = 128
LANES = 128
BF16 = jnp.bfloat16
F32 = jnp.float32
VMEM_LIMIT = 32 * 2**20
PARTS = ((1, "relay"), (1, "relay"))
ADJOINT_TILE = 2048
ADJOINT_DEPTH = 9
FORWARD_TILE = 2048
FORWARD_DEPTH = 9
FORWARD_GROUP = 1


def in_vmem():
    return pl.BlockSpec(memory_space=pltpu.VMEM)


def tile_of(width, limit):
    return max(t for t in range(LANES, min(limit, width) + 1, LANES) if width % t == 0)


def stream(k_hbm, kbuf, sem, base, steps, step, first=lambda: None):
    depth, _, group, _, ts = kbuf.shape
    groups = k_hbm.shape[1] // group
    total = steps * groups

    def copy(i):
        off = pl.multiple_of(base + i // groups * ts, LANES)
        slot = i % depth
        source = k_hbm.at[:, pl.ds(i % groups * group, group), :, pl.ds(off, ts)]
        return pltpu.make_async_copy(source, kbuf.at[slot], sem.at[slot])

    for i in range(min(depth - 1, total)):
        copy(i).start()
    first()

    def body(i, carry):
        @pl.when(i + depth - 1 < total)
        def _():
            copy(i + depth - 1).start()

        copy(i).wait()
        step(i // groups, i % groups, kbuf.at[i % depth])
        return carry

    lax.fori_loop(0, total, body, 0)


def adjoint_body(turn_ref, k_hbm, *refs, pieces, points, base, steps, stage):
    ins, refs = refs[: STAGES[stage]], refs[STAGES[stage] :]
    o_refs, refs = refs[:pieces], refs[pieces:]
    made, (kbuf, sem, scr) = refs[:-3], refs[-3:]
    _, _, _, receivers, ts = kbuf.shape
    fl = k_hbm.shape[1]
    size = 2 * points * fl // pieces
    turn = turn_ref[0]
    l_ref = made[0] if made else ins[0]

    def first():
        if stage == "rest":
            return
        if stage == "step":
            length = step_length(ins[1])
            made[2][...] = jnp.broadcast_to(length, made[2].shape)
        for f in range(fl):
            real, imag = ins[0][0, f], ins[0][1, f]
            if stage == "step":
                top = 2 * points * f
                real = real - length * ins[2][top : top + points]
                imag = imag - length * ins[2][top + points : top + 2 * points]
                made[1][0, f] = real
                made[1][1, f] = imag
            l_ref[f, :, :receivers] = jnp.concatenate([real, imag], 0).astype(BF16)
            l_ref[f, :, receivers:] = jnp.concatenate([imag, -real], 0).astype(BF16)

    def step(s, f, block):
        out = jnp.dot(l_ref[f], block[...].reshape(2 * receivers, ts), preferred_element_type=F32)
        for c in range(2):
            for j in range(ts // LANES):
                scr[j, pl.ds(c * fl + f, points, stride=2 * fl), :] = out[
                    c * points : (c + 1) * points, j * LANES : (j + 1) * LANES
                ]

        @pl.when(f == fl - 1)
        def _():
            for k, o_ref in enumerate(o_refs):
                rows = pl.ds(pl.multiple_of((turn ^ k) * size, size), size)
                for j in range(ts // LANES):
                    at = pl.ds(pl.multiple_of(s * ts + j * LANES, LANES), LANES)
                    o_ref[:, at] = scr[j, rows, :].astype(BF16)

    stream(k_hbm, kbuf, sem, base, steps, step, first)


STAGES = {"data": 1, "step": 3, "rest": 1}


def adjoint(turn, kernel, ins, stage, points, base, width, pieces):
    _, fl, receivers, sources = kernel.shape
    ts = tile_of(width, ADJOINT_TILE)
    depth = min(ADJOINT_DEPTH, width // ts * fl)
    shapes = [jax.ShapeDtypeStruct((2 * points * fl // pieces, width), BF16)] * pieces
    if stage != "rest":
        shapes.append(jax.ShapeDtypeStruct((fl, 2 * points, 2 * receivers), BF16))
    if stage == "step":
        shapes.append(jax.ShapeDtypeStruct((2, fl, points, receivers), F32))
        shapes.append(jax.ShapeDtypeStruct((8, LANES), F32))
    out = pl.pallas_call(
        functools.partial(
            adjoint_body, pieces=pieces, points=points, base=base, steps=width // ts, stage=stage
        ),
        in_specs=[pl.BlockSpec(memory_space=pltpu.SMEM), pl.BlockSpec(memory_space=pl.ANY)] + [in_vmem()] * len(ins),
        out_specs=[in_vmem()] * len(shapes),
        out_shape=shapes,
        scratch_shapes=[
            pltpu.VMEM((depth, 2, 1, receivers, ts), BF16),
            pltpu.SemaphoreType.DMA((depth,)),
            pltpu.VMEM((ts // LANES, 2 * points * fl, LANES), F32),
        ],
        compiler_params=pltpu.CompilerParams(vmem_limit_bytes=VMEM_LIMIT),
        cost_estimate=pl.CostEstimate(
            flops=64 * points * receivers * width * fl, bytes_accessed=4 * fl * receivers * width, transcendentals=0
        ),
        name="adjoint",
    )(turn, kernel, *ins)
    return out[:pieces], out[pieces:]


def forward_body(turn_ref, k_hbm, al_ref, init_ref, *refs, pieces, points, base, steps):
    d_refs, (o_ref, kbuf, sem, dscr, acc) = refs[:pieces], refs[pieces:]
    _, _, group, receivers, ts = kbuf.shape
    fl = k_hbm.shape[1]
    size = 2 * points * fl // pieces
    turn = turn_ref[0]
    acc[...] = jnp.zeros(acc.shape, F32)

    def step(s, n, block):
        tiles = range(ts // LANES)

        @pl.when(n == 0)
        def _():
            for k, d_ref in enumerate(d_refs):
                rows = pl.ds(pl.multiple_of((turn ^ k) * size, size), size)
                for j in tiles:
                    at = pl.ds(pl.multiple_of(s * ts + j * LANES, LANES), LANES)
                    dscr[j, rows, :] = d_ref[:, at].astype(F32)

        def part(c, f):
            rows = pl.ds(c * fl + n * group + f, points, stride=2 * fl)
            return jnp.concatenate([dscr[j, rows, :] for j in tiles], 1)

        field = jnp.concatenate([part(c, f) for f in range(group) for c in range(2)], 0).astype(BF16)
        acc[n] += lax.dot_general(
            field,
            block[...].reshape(2 * group * receivers, ts),
            (((1,), (1,)), ((), ())),
            preferred_element_type=F32,
        )

    stream(k_hbm, kbuf, sem, base, steps, step)
    for f in range(fl):
        n, g = divmod(f, group)
        whole = acc[n, 2 * points * g : 2 * points * (g + 1)]
        by_real = whole[:, g * receivers : (g + 1) * receivers]
        by_imag = whole[:, (group + g) * receivers : (group + g + 1) * receivers]
        top = 2 * points * f
        mid = top + points
        end = top + 2 * points
        real = by_real[:points] - by_imag[points:]
        imag = by_real[points:] + by_imag[:points]
        if init_ref is not None:
            real += init_ref[top:mid]
            imag += init_ref[mid:end]
        o_ref[top:mid] = real
        o_ref[mid:end] = imag
    extra = jnp.concatenate([al_ref[...], jnp.zeros((8, receivers - LANES), F32)], 1)
    if init_ref is not None:
        extra += init_ref[2 * points * fl :]
    o_ref[2 * points * fl :] = extra


def forward(turn, kernel, field, alignment, init, base):
    _, fl, receivers, sources = kernel.shape
    pieces = len(field)
    points = field[0].shape[0] * pieces // (2 * fl)
    width = field[0].shape[1]
    ts = tile_of(width, FORWARD_TILE)
    group = FORWARD_GROUP if fl % FORWARD_GROUP == 0 else 1
    depth = min(FORWARD_DEPTH, width // ts * fl // group)
    body = functools.partial(forward_body, pieces=pieces, points=points, base=base, steps=width // ts)
    if init is None:
        inner, start = body, []
        body = lambda turn, k, al, *rest: inner(turn, k, al, None, *rest)
    else:
        start = [init]
    specs = [pl.BlockSpec(memory_space=pltpu.SMEM), pl.BlockSpec(memory_space=pl.ANY), in_vmem()]
    return pl.pallas_call(
        body,
        in_specs=specs + [in_vmem()] * (len(start) + pieces),
        out_specs=in_vmem(),
        out_shape=jax.ShapeDtypeStruct((2 * points * fl + 8, receivers), F32),
        scratch_shapes=[
            pltpu.VMEM((depth, 2, group, receivers, ts), BF16),
            pltpu.SemaphoreType.DMA((depth,)),
            pltpu.VMEM((ts // LANES, 2 * points * fl, LANES), F32),
            pltpu.VMEM((fl // group, 2 * points * group, 2 * receivers * group), F32),
        ],
        compiler_params=pltpu.CompilerParams(vmem_limit_bytes=VMEM_LIMIT),
        cost_estimate=pl.CostEstimate(
            flops=64 * points * receivers * width * fl, bytes_accessed=4 * fl * receivers * width, transcendentals=0
        ),
        name="forward",
    )(turn, kernel, alignment, *start, *field)


def split(whole):
    high = whole.astype(BF16)
    return high, (whole - high.astype(F32)).astype(BF16)


def taper_body(t_ref, *refs, inputs, points, rows):
    g_refs, d_refs, al_ref = refs[:inputs], refs[inputs:-1], refs[-1]
    width = g_refs[0].shape[1]
    step = tile_of(width, 512)
    own = len(d_refs) * rows
    total = jnp.zeros((8, LANES), F32)
    for p in range(points):
        high, low = split(t_ref[p])
        places = [
            (ref, slice(at, at + rows)) for ref in g_refs for at in range(p * rows, ref.shape[0], points * rows)
        ]
        for at in range(0, width, step):
            cols = slice(at, at + step)
            g = jnp.concatenate([ref[place, cols] for ref, place in places], 0)
            d = jnp.dot(low, g, preferred_element_type=F32)
            d += jnp.dot(high, g, preferred_element_type=F32)
            for k, ref in enumerate(d_refs):
                ref[p * rows : (p + 1) * rows, cols] = d[k * rows : (k + 1) * rows].astype(BF16)
            product = d * g[:own].astype(F32)
            for j in range(0, step, LANES):
                total += product[:, j : j + LANES].reshape(own // 8, 8, LANES).sum(0)
    al_ref[...] = total


def taper(matrices, blocks, outputs, rows):
    points = matrices.shape[0]
    width = blocks[0].shape[1]
    return pl.pallas_call(
        functools.partial(taper_body, inputs=len(blocks), points=points, rows=rows),
        in_specs=[in_vmem()] * (1 + len(blocks)),
        out_specs=[in_vmem()] * (outputs + 1),
        out_shape=[jax.ShapeDtypeStruct((points * rows, width), BF16)] * outputs
        + [jax.ShapeDtypeStruct((8, LANES), F32)],
        compiler_params=pltpu.CompilerParams(vmem_limit_bytes=VMEM_LIMIT),
        cost_estimate=pl.CostEstimate(
            flops=6 * matrices.size * width, bytes_accessed=8 * points * rows * outputs * width, transcendentals=0
        ),
        name="taper",
    )(matrices, *blocks)


def merge_body(own_ref, got_ref, p_ref, sums_ref):
    size, receivers = p_ref.shape
    projected = own_ref[:size] + got_ref[:size]
    p_ref[...] = projected
    squares = jnp.sum((projected * projected).reshape(size // 8, 8, receivers), 0)
    pad = -receivers % LANES
    if pad:
        squares = jnp.concatenate([squares, jnp.zeros((8, pad), F32)], 1)
    curvature = sum(squares[:, j : j + LANES] for j in range(0, receivers + pad, LANES))
    alignment = own_ref[size:, :LANES] + got_ref[size:, :LANES]
    for at in range(0, sums_ref.shape[0], 16):
        sums_ref[at : at + 8] = alignment
        sums_ref[at + 8 : at + 16] = curvature


def merge(own, got, count):
    size, receivers = own.shape
    return pl.pallas_call(
        merge_body,
        in_specs=[in_vmem()] * 2,
        out_specs=[in_vmem()] * 2,
        out_shape=[jax.ShapeDtypeStruct((size - 8, receivers), F32), jax.ShapeDtypeStruct((16 * count, LANES), F32)],
        name="merge",
    )(own, got)


def wave_table(freqs, fl):
    samples = np.arange(NT)[:, None]
    phase = (samples * np.arange(freqs)[None, :] % NT) * (2.0 * math.pi / NT)
    table = np.stack([np.cos(phase), -np.sin(phase)], 1) * freqs**-0.5
    table = table.reshape(NT, 2, freqs // fl, fl).transpose(0, 2, 1, 3)
    return table.reshape(NT, 2 * freqs).astype(np.float32)


def swap(x):
    return lax.ppermute(x, "src", [(0, 1), (1, 0)])


def step_length(s_ref):
    sums = sum(s_ref[at : at + 16] for at in range(0, s_ref.shape[0], 16))
    return jnp.sum(sums[0:8], keepdims=True) / jnp.sum(sums[8:16], keepdims=True)


def finish_body(place_ref, s_ref, p_ref, r_ref, *refs, spans, pieces):
    earlier, fields, (e_hbm, out_ref, stage, scr, sem) = refs[: ITERS - 1], refs[ITERS - 1 : -5], refs[-5:]
    _, fl, points, share = out_ref.shape
    lengths = [ref[0:1, 0:1] for ref in earlier] + [step_length(s_ref)]
    copies = []
    at = 0
    for part, ((base, width), count) in enumerate(zip(spans, pieces)):
        size = 2 * points * fl // count
        turn = place_ref[1 + part]

        def one(i, carry, at=at, base=base, count=count, size=size, turn=turn):
            off = pl.multiple_of(i * LANES, LANES)
            out = pl.ds(pl.multiple_of(base + i * LANES, LANES), LANES)
            for k in range(count):
                values = [fields[at + n * count + k][:, pl.ds(off, LANES)].astype(F32) for n in range(ITERS)]
                rows = pl.ds(pl.multiple_of((turn ^ k) * size, size), size)
                scr[i % 2, rows, :] = sum(a * x for a, x in zip(lengths, values))
            for c in range(2):
                for f in range(fl):
                    stage[c, f, :, out] = scr[i % 2, pl.ds(c * fl + f, points, stride=2 * fl), :]
            return carry

        lax.fori_loop(0, width // LANES, one, 0, unroll=2)
        span = pl.ds(base, width)
        copies.append(
            pltpu.make_async_copy(stage.at[:, :, :, span], e_hbm.at[:, :, :, span], sem.at[part])
        )
        copies[-1].start()
        at += ITERS * count
    for c in range(2):
        for f in range(fl):
            top = (2 * f + c) * points
            residual = r_ref[c, f] - lengths[-1] * p_ref[top : top + points]
            mine = residual[:, :share]
            for n in range(1, residual.shape[1] // share):
                mine = jnp.where(place_ref[0] == n, residual[:, n * share : (n + 1) * share], mine)
            out_ref[c, f] = mine
    for copy in copies:
        copy.wait()


def finish(core, turns, sums, projected, residual, lengths, fields, spans, fl, points, share):
    parts = range(len(spans))
    flat = [x for part in parts for field in fields for x in field[part]]
    shape = (2, fl, points, sum(width for _, width in spans))
    return pl.pallas_call(
        functools.partial(finish_body, spans=spans, pieces=[len(fields[0][part]) for part in parts]),
        in_specs=[pl.BlockSpec(memory_space=pltpu.SMEM)] + [in_vmem()] * (3 + len(lengths) + len(flat)),
        out_specs=[pl.BlockSpec(memory_space=pl.ANY), in_vmem()],
        out_shape=[jax.ShapeDtypeStruct(shape, F32), jax.ShapeDtypeStruct((2, fl, points, share), F32)],
        scratch_shapes=[
            pltpu.VMEM(shape, F32),
            pltpu.VMEM((2, 2 * points * fl, LANES), F32),
            pltpu.SemaphoreType.DMA((len(spans),)),
        ],
        compiler_params=pltpu.CompilerParams(vmem_limit_bytes=VMEM_LIMIT),
        name="finish",
    )(jnp.concatenate([core] + turns), sums, projected, residual, *lengths, *flat)


def then(x, *earlier):
    return lax.optimization_barrier((x, *earlier))[0]


def send(x, hop):
    return lax.ppermute(x, "freq", [(i, i ^ hop) for i in range(lax.axis_size("freq"))])


def exchange(x, rows):
    width = x.shape[-1]
    return lax.all_to_all(x.reshape(-1, rows, width), "freq", 0, 0, tiled=True).reshape(-1, width)


def body(kernel, data, win_start, win_end):
    count = lax.axis_size("freq")
    src_count = lax.axis_size("src")
    _, fl, receivers, sources = kernel.shape
    points = data.shape[3]
    rows = 2 * fl
    me = lax.axis_index("freq")
    own = points // count
    permutes = count & (count - 1) == 0 and rows % 16 == 0 and own == 1
    inner = {"plain": 1, "direct": 1, "relay": 2}
    parts, base = [], 0
    for weight, mode in PARTS:
        width = sources * weight // sum(w for w, _ in PARTS)
        parts.append((base, width, mode if permutes else "plain"))
        base += width

    def turn_of(mode):
        turn = (me // inner[mode]).reshape(1).astype(jnp.int32)
        return jnp.zeros_like(turn) if mode == "plain" else turn

    def pieces_of(mode):
        return 1 if mode == "plain" else count // inner[mode]

    table = jnp.asarray(wave_table(fl * count, fl))
    samples = jnp.arange(NT, dtype=jnp.int32)[None, :]

    def matrices_of(mode):
        size = own * inner[mode]
        first = me // inner[mode] * size
        starts = lax.dynamic_slice_in_dim(win_start, first, size)[:, None]
        ends = lax.dynamic_slice_in_dim(win_end, first, size)[:, None]
        window = ((samples >= starts) & (samples < ends)).astype(F32)
        right = table
        if mode != "plain":
            blocks = table.reshape(NT, count, rows)
            order = [me ^ (k * inner[mode] + y) for y in range(inner[mode]) for k in range(pieces_of(mode))]
            right = jnp.concatenate([lax.dynamic_index_in_dim(blocks, b, 1, keepdims=False) for b in order], 1)
        left = right[:, : right.shape[1] // inner[mode]]
        return jnp.einsum("pta,tb->pab", window[:, :, None] * left, right, precision=lax.Precision.HIGHEST)

    matrices = {mode: matrices_of(mode) for mode in sorted({mode for _, _, mode in parts})}

    def scatter(blocks, mode):
        if mode == "plain":
            return [exchange(blocks[0], rows)]
        return [blocks[0]] + [send(blocks[k], k * inner[mode]) for k in range(1, len(blocks))]

    def pair_up(got, mode):
        if mode != "relay":
            return got
        joined = jnp.concatenate(got, 0)
        return [joined, send(joined, 1)]

    def tapered(got, mode):
        if mode != "plain":
            *field, alignment = taper(matrices[mode], got, pieces_of(mode), rows)
            return field, alignment
        if own == 1:
            field, alignment = taper(matrices[mode], got, 1, count * rows)
            return [field], alignment
        width = got[0].shape[-1]
        got = got[0].reshape(count, own, rows, width)
        done = [
            taper(matrices[mode][p : p + 1], [got[:, p].reshape(-1, width)], 1, count * rows) for p in range(own)
        ]
        field = jnp.stack([d.reshape(count, rows, width) for d, _ in done], 1).reshape(-1, width)
        return [field], sum(a for _, a in done)

    residual = data.transpose(0, 1, 3, 2)
    lengths, fields = [], []
    for iteration in range(ITERS):
        image = None
        fields.append([])
        gradients, gathered, sent = [], [], []
        if iteration == 0:
            stage, ins = "data", [residual]
        else:
            stage, ins = "step", [residual, sums, projected]
        for base, width, mode in parts:
            gradient, made = adjoint(turn_of(mode), kernel, ins, stage, points, base, width, pieces_of(mode))
            if stage == "step":
                residual = made[1]
                lengths.append(made[2])
            if made:
                lhs = made[0]
            stage, ins = "rest", [then(lhs, gradient[-1])]
            gradients.append(gradient)
            if gathered and mode == "relay":
                gradient = list(gradient[:2]) + [then(x, gathered[-1][0]) for x in gradient[2:]]
            gathered.append(pair_up(scatter(gradient, mode), mode))
        for n, (_, _, mode) in enumerate(parts):
            got = gathered[n]
            if n + 1 < len(parts):
                got = [then(got[0], gradients[n + 1][-1])] + got[1:]
            field, alignment = tapered(got, mode)
            if sent and mode == "relay":
                field = list(field[:2]) + [then(x, sent[-1][1][len(field) // 2]) for x in field[2:]]
            sent.append((field, scatter(field, mode), alignment))
        for n, (base, _, mode) in enumerate(parts):
            _, field, alignment = sent[n]
            if n + 1 < len(parts):
                field = [then(field[0], sent[n + 1][0][-1])] + field[1:]
            image = forward(turn_of(mode), kernel, field, alignment, image, base)
            fields[-1].append(field)
        got = swap(image) if src_count == 2 else lax.psum(image, "src") - image
        projected, sums = merge(image, got, count)
        sums = exchange(sums, 16)
    spans = [(base, width) for base, width, _ in parts]
    turns = [turn_of(mode) for _, _, mode in parts]
    core = lax.axis_index("src").reshape(1).astype(jnp.int32)
    share = receivers // src_count
    estimate, residual = finish(
        core, turns, sums, projected, residual, lengths, fields, spans, fl, points, share
    )
    return estimate, residual.transpose(0, 1, 3, 2)


def solution(mesh):
    in_specs = (P("grp", "freq", None, "src"), P("grp", "freq", None, None), P("grp"), P("grp"))
    out_specs = (P("grp", "freq", None, "src"), P("grp", "freq", "src", None))
    return jax.shard_map(body, mesh=mesh, in_specs=in_specs, out_specs=out_specs, check_vma=False)
```

```python
import functools
import math

import jax
import jax.numpy as jnp
import numpy as np
from jax import lax
from jax.experimental import pallas as pl
from jax.experimental.pallas import tpu as pltpu
from jax.sharding import PartitionSpec as P

ITERS = 2
NT = 128
LANES = 128
BF16 = jnp.bfloat16
F32 = jnp.float32
VMEM_LIMIT = 32 * 2**20
PARTS = ((1, "relay"), (1, "relay"))
ADJOINT_TILE = 2048
ADJOINT_DEPTH = 9
FORWARD_TILE = 2048
FORWARD_DEPTH = 9
FORWARD_GROUP = 1


def in_vmem():
    return pl.BlockSpec(memory_space=pltpu.VMEM)


def tile_of(width, limit):
    return max(t for t in range(LANES, min(limit, width) + 1, LANES) if width % t == 0)


def stream(k_hbm, kbuf, sem, base, steps, step, first=lambda: None):
    depth, _, group, _, ts = kbuf.shape
    groups = k_hbm.shape[1] // group
    total = steps * groups

    def copy(i):
        off = pl.multiple_of(base + i // groups * ts, LANES)
        slot = i % depth
        source = k_hbm.at[:, pl.ds(i % groups * group, group), :, pl.ds(off, ts)]
        return pltpu.make_async_copy(source, kbuf.at[slot], sem.at[slot])

    for i in range(min(depth - 1, total)):
        copy(i).start()
    first()

    def body(i, carry):
        @pl.when(i + depth - 1 < total)
        def _():
            copy(i + depth - 1).start()

        copy(i).wait()
        step(i // groups, i % groups, kbuf.at[i % depth])
        return carry

    lax.fori_loop(0, total, body, 0)


def adjoint_body(turn_ref, k_hbm, *refs, pieces, points, base, steps, stage):
    ins, refs = refs[: STAGES[stage]], refs[STAGES[stage] :]
    o_refs, refs = refs[:pieces], refs[pieces:]
    made, (kbuf, sem, scr) = refs[:-3], refs[-3:]
    _, _, _, receivers, ts = kbuf.shape
    fl = k_hbm.shape[1]
    size = 2 * points * fl // pieces
    turn = turn_ref[0]
    l_ref = made[0] if made else ins[0]

    def first():
        if stage == "rest":
            return
        if stage == "step":
            length = step_length(ins[1])
            made[2][...] = jnp.broadcast_to(length, made[2].shape)
        for f in range(fl):
            real, imag = ins[0][0, f], ins[0][1, f]
            if stage == "step":
                top = 2 * points * f
                real = real - length * ins[2][top : top + points]
                imag = imag - length * ins[2][top + points : top + 2 * points]
                made[1][0, f] = real
                made[1][1, f] = imag
            l_ref[f, :, :receivers] = jnp.concatenate([real, imag], 0).astype(BF16)
            l_ref[f, :, receivers:] = jnp.concatenate([imag, -real], 0).astype(BF16)

    def step(s, f, block):
        out = jnp.dot(l_ref[f], block[...].reshape(2 * receivers, ts), preferred_element_type=F32)
        for c in range(2):
            for j in range(ts // LANES):
                scr[j, pl.ds(c * fl + f, points, stride=2 * fl), :] = out[
                    c * points : (c + 1) * points, j * LANES : (j + 1) * LANES
                ]

        @pl.when(f == fl - 1)
        def _():
            for k, o_ref in enumerate(o_refs):
                rows = pl.ds(pl.multiple_of((turn ^ k) * size, size), size)
                for j in range(ts // LANES):
                    at = pl.ds(pl.multiple_of(s * ts + j * LANES, LANES), LANES)
                    o_ref[:, at] = scr[j, rows, :].astype(BF16)

    stream(k_hbm, kbuf, sem, base, steps, step, first)


STAGES = {"data": 1, "step": 3, "rest": 1}


def adjoint(turn, kernel, ins, stage, points, base, width, pieces):
    _, fl, receivers, sources = kernel.shape
    ts = tile_of(width, ADJOINT_TILE)
    depth = min(ADJOINT_DEPTH, width // ts * fl)
    shapes = [jax.ShapeDtypeStruct((2 * points * fl // pieces, width), BF16)] * pieces
    if stage != "rest":
        shapes.append(jax.ShapeDtypeStruct((fl, 2 * points, 2 * receivers), BF16))
    if stage == "step":
        shapes.append(jax.ShapeDtypeStruct((2, fl, points, receivers), F32))
        shapes.append(jax.ShapeDtypeStruct((8, LANES), F32))
    out = pl.pallas_call(
        functools.partial(
            adjoint_body, pieces=pieces, points=points, base=base, steps=width // ts, stage=stage
        ),
        in_specs=[pl.BlockSpec(memory_space=pltpu.SMEM), pl.BlockSpec(memory_space=pl.ANY)] + [in_vmem()] * len(ins),
        out_specs=[in_vmem()] * len(shapes),
        out_shape=shapes,
        scratch_shapes=[
            pltpu.VMEM((depth, 2, 1, receivers, ts), BF16),
            pltpu.SemaphoreType.DMA((depth,)),
            pltpu.VMEM((ts // LANES, 2 * points * fl + 2 * fl, LANES), F32),
        ],
        compiler_params=pltpu.CompilerParams(vmem_limit_bytes=VMEM_LIMIT),
        cost_estimate=pl.CostEstimate(
            flops=64 * points * receivers * width * fl, bytes_accessed=4 * fl * receivers * width, transcendentals=0
        ),
        name="adjoint",
    )(turn, kernel, *ins)
    return out[:pieces], out[pieces:]


def forward_body(turn_ref, k_hbm, al_ref, init_ref, *refs, pieces, points, base, steps):
    d_refs, (o_ref, kbuf, sem, dscr, acc) = refs[:pieces], refs[pieces:]
    _, _, group, receivers, ts = kbuf.shape
    fl = k_hbm.shape[1]
    size = 2 * points * fl // pieces
    turn = turn_ref[0]
    acc[...] = jnp.zeros(acc.shape, F32)

    def step(s, n, block):
        tiles = range(ts // LANES)

        @pl.when(n == 0)
        def _():
            for k, d_ref in enumerate(d_refs):
                rows = pl.ds(pl.multiple_of((turn ^ k) * size, size), size)
                for j in tiles:
                    at = pl.ds(pl.multiple_of(s * ts + j * LANES, LANES), LANES)
                    dscr[j, rows, :] = d_ref[:, at].astype(F32)

        def part(c, f):
            rows = pl.ds(c * fl + n * group + f, points, stride=2 * fl)
            return jnp.concatenate([dscr[j, rows, :] for j in tiles], 1)

        field = jnp.concatenate([part(c, f) for f in range(group) for c in range(2)], 0).astype(BF16)
        acc[n] += lax.dot_general(
            field,
            block[...].reshape(2 * group * receivers, ts),
            (((1,), (1,)), ((), ())),
            preferred_element_type=F32,
        )

    stream(k_hbm, kbuf, sem, base, steps, step)
    for f in range(fl):
        n, g = divmod(f, group)
        whole = acc[n, 2 * points * g : 2 * points * (g + 1)]
        by_real = whole[:, g * receivers : (g + 1) * receivers]
        by_imag = whole[:, (group + g) * receivers : (group + g + 1) * receivers]
        top = 2 * points * f
        mid = top + points
        end = top + 2 * points
        real = by_real[:points] - by_imag[points:]
        imag = by_real[points:] + by_imag[:points]
        if init_ref is not None:
            real += init_ref[top:mid]
            imag += init_ref[mid:end]
        o_ref[top:mid] = real
        o_ref[mid:end] = imag
    extra = jnp.concatenate([al_ref[...], jnp.zeros((8, receivers - LANES), F32)], 1)
    if init_ref is not None:
        extra += init_ref[2 * points * fl :]
    o_ref[2 * points * fl :] = extra


def forward(turn, kernel, field, alignment, init, base):
    _, fl, receivers, sources = kernel.shape
    pieces = len(field)
    points = field[0].shape[0] * pieces // (2 * fl)
    width = field[0].shape[1]
    ts = tile_of(width, FORWARD_TILE)
    group = FORWARD_GROUP if fl % FORWARD_GROUP == 0 else 1
    depth = min(FORWARD_DEPTH, width // ts * fl // group)
    body = functools.partial(forward_body, pieces=pieces, points=points, base=base, steps=width // ts)
    if init is None:
        inner, start = body, []
        body = lambda turn, k, al, *rest: inner(turn, k, al, None, *rest)
    else:
        start = [init]
    specs = [pl.BlockSpec(memory_space=pltpu.SMEM), pl.BlockSpec(memory_space=pl.ANY), in_vmem()]
    return pl.pallas_call(
        body,
        in_specs=specs + [in_vmem()] * (len(start) + pieces),
        out_specs=in_vmem(),
        out_shape=jax.ShapeDtypeStruct((2 * points * fl + 8, receivers), F32),
        scratch_shapes=[
            pltpu.VMEM((depth, 2, group, receivers, ts), BF16),
            pltpu.SemaphoreType.DMA((depth,)),
            pltpu.VMEM((ts // LANES, 2 * points * fl + 2 * fl, LANES), F32),
            pltpu.VMEM((fl // group, 2 * points * group, 2 * receivers * group), F32),
        ],
        compiler_params=pltpu.CompilerParams(vmem_limit_bytes=VMEM_LIMIT),
        cost_estimate=pl.CostEstimate(
            flops=64 * points * receivers * width * fl, bytes_accessed=4 * fl * receivers * width, transcendentals=0
        ),
        name="forward",
    )(turn, kernel, alignment, *start, *field)


def split(whole):
    high = whole.astype(BF16)
    return high, (whole - high.astype(F32)).astype(BF16)


def taper_body(t_ref, *refs, inputs, points, rows):
    g_refs, d_refs, al_ref = refs[:inputs], refs[inputs:-1], refs[-1]
    width = g_refs[0].shape[1]
    step = tile_of(width, 512)
    own = len(d_refs) * rows
    total = jnp.zeros((8, LANES), F32)
    for p in range(points):
        high, low = split(t_ref[p])
        places = [
            (ref, slice(at, at + rows)) for ref in g_refs for at in range(p * rows, ref.shape[0], points * rows)
        ]
        for at in range(0, width, step):
            cols = slice(at, at + step)
            g = jnp.concatenate([ref[place, cols] for ref, place in places], 0)
            d = jnp.dot(low, g, preferred_element_type=F32)
            d += jnp.dot(high, g, preferred_element_type=F32)
            for k, ref in enumerate(d_refs):
                ref[p * rows : (p + 1) * rows, cols] = d[k * rows : (k + 1) * rows].astype(BF16)
            product = d * g[:own].astype(F32)
            for j in range(0, step, LANES):
                total += product[:, j : j + LANES].reshape(own // 8, 8, LANES).sum(0)
    al_ref[...] = total


def taper(matrices, blocks, outputs, rows):
    points = matrices.shape[0]
    width = blocks[0].shape[1]
    return pl.pallas_call(
        functools.partial(taper_body, inputs=len(blocks), points=points, rows=rows),
        in_specs=[in_vmem()] * (1 + len(blocks)),
        out_specs=[in_vmem()] * (outputs + 1),
        out_shape=[jax.ShapeDtypeStruct((points * rows, width), BF16)] * outputs
        + [jax.ShapeDtypeStruct((8, LANES), F32)],
        compiler_params=pltpu.CompilerParams(vmem_limit_bytes=VMEM_LIMIT),
        cost_estimate=pl.CostEstimate(
            flops=6 * matrices.size * width, bytes_accessed=8 * points * rows * outputs * width, transcendentals=0
        ),
        name="taper",
    )(matrices, *blocks)


def merge_body(own_ref, got_ref, p_ref, sums_ref):
    size, receivers = p_ref.shape
    projected = own_ref[:size] + got_ref[:size]
    p_ref[...] = projected
    squares = jnp.sum((projected * projected).reshape(size // 8, 8, receivers), 0)
    pad = -receivers % LANES
    if pad:
        squares = jnp.concatenate([squares, jnp.zeros((8, pad), F32)], 1)
    curvature = sum(squares[:, j : j + LANES] for j in range(0, receivers + pad, LANES))
    alignment = own_ref[size:, :LANES] + got_ref[size:, :LANES]
    for at in range(0, sums_ref.shape[0], 16):
        sums_ref[at : at + 8] = alignment
        sums_ref[at + 8 : at + 16] = curvature


def merge(own, got, count):
    size, receivers = own.shape
    return pl.pallas_call(
        merge_body,
        in_specs=[in_vmem()] * 2,
        out_specs=[in_vmem()] * 2,
        out_shape=[jax.ShapeDtypeStruct((size - 8, receivers), F32), jax.ShapeDtypeStruct((16 * count, LANES), F32)],
        name="merge",
    )(own, got)


def wave_table(freqs, fl):
    samples = np.arange(NT)[:, None]
    phase = (samples * np.arange(freqs)[None, :] % NT) * (2.0 * math.pi / NT)
    table = np.stack([np.cos(phase), -np.sin(phase)], 1) * freqs**-0.5
    table = table.reshape(NT, 2, freqs // fl, fl).transpose(0, 2, 1, 3)
    return table.reshape(NT, 2 * freqs).astype(np.float32)


def swap(x):
    return lax.ppermute(x, "src", [(0, 1), (1, 0)])


def step_length(s_ref):
    sums = sum(s_ref[at : at + 16] for at in range(0, s_ref.shape[0], 16))
    return jnp.sum(sums[0:8], keepdims=True) / jnp.sum(sums[8:16], keepdims=True)


def finish_body(place_ref, s_ref, p_ref, r_ref, *refs, spans, pieces):
    earlier, fields, (e_hbm, out_ref, stage, scr, sem) = refs[: ITERS - 1], refs[ITERS - 1 : -5], refs[-5:]
    _, fl, points, share = out_ref.shape
    lengths = [ref[0:1, 0:1] for ref in earlier] + [step_length(s_ref)]
    copies = []
    at = 0
    for part, ((base, width), count) in enumerate(zip(spans, pieces)):
        size = 2 * points * fl // count
        turn = place_ref[1 + part]

        def one(i, carry, at=at, base=base, count=count, size=size, turn=turn):
            off = pl.multiple_of(i * LANES, LANES)
            out = pl.ds(pl.multiple_of(base + i * LANES, LANES), LANES)
            for k in range(count):
                values = [fields[at + n * count + k][:, pl.ds(off, LANES)].astype(F32) for n in range(ITERS)]
                rows = pl.ds(pl.multiple_of((turn ^ k) * size, size), size)
                scr[i % 2, rows, :] = sum(a * x for a, x in zip(lengths, values))
            for c in range(2):
                for f in range(fl):
                    stage[c, f, :, out] = scr[i % 2, pl.ds(c * fl + f, points, stride=2 * fl), :]
            return carry

        lax.fori_loop(0, width // LANES, one, 0, unroll=4)
        span = pl.ds(base, width)
        copies.append(
            pltpu.make_async_copy(stage.at[:, :, :, span], e_hbm.at[:, :, :, span], sem.at[part])
        )
        copies[-1].start()
        at += ITERS * count
    for c in range(2):
        for f in range(fl):
            top = (2 * f + c) * points
            residual = r_ref[c, f] - lengths[-1] * p_ref[top : top + points]
            mine = residual[:, :share]
            for n in range(1, residual.shape[1] // share):
                mine = jnp.where(place_ref[0] == n, residual[:, n * share : (n + 1) * share], mine)
            out_ref[c, f] = mine
    for copy in copies:
        copy.wait()


def finish(core, turns, sums, projected, residual, lengths, fields, spans, fl, points, share):
    parts = range(len(spans))
    flat = [x for part in parts for field in fields for x in field[part]]
    shape = (2, fl, points, sum(width for _, width in spans))
    return pl.pallas_call(
        functools.partial(finish_body, spans=spans, pieces=[len(fields[0][part]) for part in parts]),
        in_specs=[pl.BlockSpec(memory_space=pltpu.SMEM)] + [in_vmem()] * (3 + len(lengths) + len(flat)),
        out_specs=[pl.BlockSpec(memory_space=pl.ANY), in_vmem()],
        out_shape=[jax.ShapeDtypeStruct(shape, F32), jax.ShapeDtypeStruct((2, fl, points, share), F32)],
        scratch_shapes=[
            pltpu.VMEM(shape, F32),
            pltpu.VMEM((2, 2 * points * fl + 2 * fl, LANES), F32),
            pltpu.SemaphoreType.DMA((len(spans),)),
        ],
        compiler_params=pltpu.CompilerParams(vmem_limit_bytes=VMEM_LIMIT),
        name="finish",
    )(jnp.concatenate([core] + turns), sums, projected, residual, *lengths, *flat)


def then(x, *earlier):
    return lax.optimization_barrier((x, *earlier))[0]


def send(x, hop):
    return lax.ppermute(x, "freq", [(i, i ^ hop) for i in range(lax.axis_size("freq"))])


def exchange(x, rows):
    width = x.shape[-1]
    return lax.all_to_all(x.reshape(-1, rows, width), "freq", 0, 0, tiled=True).reshape(-1, width)


def body(kernel, data, win_start, win_end):
    count = lax.axis_size("freq")
    src_count = lax.axis_size("src")
    _, fl, receivers, sources = kernel.shape
    points = data.shape[3]
    rows = 2 * fl
    me = lax.axis_index("freq")
    own = points // count
    permutes = count & (count - 1) == 0 and rows % 16 == 0 and own == 1
    inner = {"plain": 1, "direct": 1, "relay": 2}
    parts, base = [], 0
    for weight, mode in PARTS:
        width = sources * weight // sum(w for w, _ in PARTS)
        parts.append((base, width, mode if permutes else "plain"))
        base += width

    def turn_of(mode):
        turn = (me // inner[mode]).reshape(1).astype(jnp.int32)
        return jnp.zeros_like(turn) if mode == "plain" else turn

    def pieces_of(mode):
        return 1 if mode == "plain" else count // inner[mode]

    table = jnp.asarray(wave_table(fl * count, fl))
    samples = jnp.arange(NT, dtype=jnp.int32)[None, :]

    def matrices_of(mode):
        size = own * inner[mode]
        first = me // inner[mode] * size
        starts = lax.dynamic_slice_in_dim(win_start, first, size)[:, None]
        ends = lax.dynamic_slice_in_dim(win_end, first, size)[:, None]
        window = ((samples >= starts) & (samples < ends)).astype(F32)
        right = table
        if mode != "plain":
            blocks = table.reshape(NT, count, rows)
            order = [me ^ (k * inner[mode] + y) for y in range(inner[mode]) for k in range(pieces_of(mode))]
            right = jnp.concatenate([lax.dynamic_index_in_dim(blocks, b, 1, keepdims=False) for b in order], 1)
        left = right[:, : right.shape[1] // inner[mode]]
        return jnp.einsum("pta,tb->pab", window[:, :, None] * left, right, precision=lax.Precision.HIGHEST)

    matrices = {mode: matrices_of(mode) for mode in sorted({mode for _, _, mode in parts})}

    def scatter(blocks, mode):
        if mode == "plain":
            return [exchange(blocks[0], rows)]
        return [blocks[0]] + [send(blocks[k], k * inner[mode]) for k in range(1, len(blocks))]

    def pair_up(got, mode):
        if mode != "relay":
            return got
        joined = jnp.concatenate(got, 0)
        return [joined, send(joined, 1)]

    def tapered(got, mode):
        if mode != "plain":
            *field, alignment = taper(matrices[mode], got, pieces_of(mode), rows)
            return field, alignment
        if own == 1:
            field, alignment = taper(matrices[mode], got, 1, count * rows)
            return [field], alignment
        width = got[0].shape[-1]
        got = got[0].reshape(count, own, rows, width)
        done = [
            taper(matrices[mode][p : p + 1], [got[:, p].reshape(-1, width)], 1, count * rows) for p in range(own)
        ]
        field = jnp.stack([d.reshape(count, rows, width) for d, _ in done], 1).reshape(-1, width)
        return [field], sum(a for _, a in done)

    residual = data.transpose(0, 1, 3, 2)
    lengths, fields = [], []
    for iteration in range(ITERS):
        image = None
        fields.append([])
        gradients, gathered, sent = [], [], []
        if iteration == 0:
            stage, ins = "data", [residual]
        else:
            stage, ins = "step", [residual, sums, projected]
        for base, width, mode in parts:
            gradient, made = adjoint(turn_of(mode), kernel, ins, stage, points, base, width, pieces_of(mode))
            if stage == "step":
                residual = made[1]
                lengths.append(made[2])
            if made:
                lhs = made[0]
            stage, ins = "rest", [then(lhs, gradient[-1])]
            gradients.append(gradient)
            if gathered and mode == "relay":
                gradient = list(gradient[:2]) + [then(x, gathered[-1][0]) for x in gradient[2:]]
            gathered.append(pair_up(scatter(gradient, mode), mode))
        for n, (_, _, mode) in enumerate(parts):
            got = gathered[n]
            if n + 1 < len(parts):
                got = [then(got[0], gradients[n + 1][-1])] + got[1:]
            field, alignment = tapered(got, mode)
            if sent and mode == "relay":
                field = list(field[:2]) + [then(x, sent[-1][1][len(field) // 2]) for x in field[2:]]
            sent.append((field, scatter(field, mode), alignment))
        for n, (base, _, mode) in enumerate(parts):
            _, field, alignment = sent[n]
            if n + 1 < len(parts):
                field = [then(field[0], sent[n + 1][0][-1])] + field[1:]
            image = forward(turn_of(mode), kernel, field, alignment, image, base)
            fields[-1].append(field)
        got = swap(image) if src_count == 2 else lax.psum(image, "src") - image
        projected, sums = merge(image, got, count)
        sums = exchange(sums, 16)
    spans = [(base, width) for base, width, _ in parts]
    turns = [turn_of(mode) for _, _, mode in parts]
    core = lax.axis_index("src").reshape(1).astype(jnp.int32)
    share = receivers // src_count
    estimate, residual = finish(
        core, turns, sums, projected, residual, lengths, fields, spans, fl, points, share
    )
    return estimate, residual.transpose(0, 1, 3, 2)


def solution(mesh):
    in_specs = (P("grp", "freq", None, "src"), P("grp", "freq", None, None), P("grp"), P("grp"))
    out_specs = (P("grp", "freq", None, "src"), P("grp", "freq", "src", None))
    return jax.shard_map(body, mesh=mesh, in_specs=in_specs, out_specs=out_specs, check_vma=False)
```

```python
import functools
import math

import jax
import jax.numpy as jnp
import numpy as np
from jax import lax
from jax.experimental import pallas as pl
from jax.experimental.pallas import tpu as pltpu
from jax.sharding import PartitionSpec as P

ITERS = 2
NT = 128
LANES = 128
BF16 = jnp.bfloat16
F32 = jnp.float32
VMEM_LIMIT = 32 * 2**20
PARTS = ((1, "relay"), (1, "relay"))
ADJOINT_TILE = 2048
ADJOINT_DEPTH = 9
FORWARD_TILE = 2048
FORWARD_DEPTH = 9
FORWARD_GROUP = 1


def in_vmem():
    return pl.BlockSpec(memory_space=pltpu.VMEM)


def tile_of(width, limit):
    return max(t for t in range(LANES, min(limit, width) + 1, LANES) if width % t == 0)


def stream(k_hbm, kbuf, sem, base, steps, step, first=lambda: None):
    depth, _, group, _, ts = kbuf.shape
    groups = k_hbm.shape[1] // group
    total = steps * groups

    def copy(i):
        off = pl.multiple_of(base + i // groups * ts, LANES)
        slot = i % depth
        source = k_hbm.at[:, pl.ds(i % groups * group, group), :, pl.ds(off, ts)]
        return pltpu.make_async_copy(source, kbuf.at[slot], sem.at[slot])

    for i in range(min(depth - 1, total)):
        copy(i).start()
    first()

    def body(i, carry):
        @pl.when(i + depth - 1 < total)
        def _():
            copy(i + depth - 1).start()

        copy(i).wait()
        step(i // groups, i % groups, kbuf.at[i % depth])
        return carry

    lax.fori_loop(0, total, body, 0)


def adjoint_body(turn_ref, k_hbm, *refs, pieces, points, base, steps, stage):
    ins, refs = refs[: STAGES[stage]], refs[STAGES[stage] :]
    o_refs, refs = refs[:pieces], refs[pieces:]
    made, (kbuf, sem, scr) = refs[:-3], refs[-3:]
    _, _, _, receivers, ts = kbuf.shape
    fl = k_hbm.shape[1]
    size = 2 * points * fl // pieces
    turn = turn_ref[0]
    l_ref = made[0] if made else ins[0]

    def first():
        if stage == "rest":
            return
        if stage == "step":
            length = step_length(ins[1])
            made[2][...] = jnp.broadcast_to(length, made[2].shape)
        for f in range(fl):
            real, imag = ins[0][0, f], ins[0][1, f]
            if stage == "step":
                top = 2 * points * f
                real = real - length * ins[2][top : top + points]
                imag = imag - length * ins[2][top + points : top + 2 * points]
                made[1][0, f] = real
                made[1][1, f] = imag
            l_ref[f, :, :receivers] = jnp.concatenate([real, imag], 0).astype(BF16)
            l_ref[f, :, receivers:] = jnp.concatenate([imag, -real], 0).astype(BF16)

    def step(s, f, block):
        out = jnp.dot(l_ref[f], block[...].reshape(2 * receivers, ts), preferred_element_type=F32)
        for c in range(2):
            for j in range(ts // LANES):
                scr[j, pl.ds(c * fl + f, points, stride=2 * fl), :] = out[
                    c * points : (c + 1) * points, j * LANES : (j + 1) * LANES
                ]

        @pl.when(f == fl - 1)
        def _():
            for k, o_ref in enumerate(o_refs):
                rows = pl.ds(pl.multiple_of((turn ^ k) * size, size), size)
                for j in range(ts // LANES):
                    at = pl.ds(pl.multiple_of(s * ts + j * LANES, LANES), LANES)
                    o_ref[:, at] = scr[j, rows, :].astype(BF16)

    stream(k_hbm, kbuf, sem, base, steps, step, first)


STAGES = {"data": 1, "step": 3, "rest": 1}


def adjoint(turn, kernel, ins, stage, points, base, width, pieces):
    _, fl, receivers, sources = kernel.shape
    ts = tile_of(width, ADJOINT_TILE)
    depth = min(ADJOINT_DEPTH, width // ts * fl)
    shapes = [jax.ShapeDtypeStruct((2 * points * fl // pieces, width), BF16)] * pieces
    if stage != "rest":
        shapes.append(jax.ShapeDtypeStruct((fl, 2 * points, 2 * receivers), BF16))
    if stage == "step":
        shapes.append(jax.ShapeDtypeStruct((2, fl, points, receivers), F32))
        shapes.append(jax.ShapeDtypeStruct((8, LANES), F32))
    out = pl.pallas_call(
        functools.partial(
            adjoint_body, pieces=pieces, points=points, base=base, steps=width // ts, stage=stage
        ),
        in_specs=[pl.BlockSpec(memory_space=pltpu.SMEM), pl.BlockSpec(memory_space=pl.ANY)] + [in_vmem()] * len(ins),
        out_specs=[in_vmem()] * len(shapes),
        out_shape=shapes,
        scratch_shapes=[
            pltpu.VMEM((depth, 2, 1, receivers, ts), BF16),
            pltpu.SemaphoreType.DMA((depth,)),
            pltpu.VMEM((ts // LANES, 2 * points * fl + 2 * fl, LANES), F32),
        ],
        compiler_params=pltpu.CompilerParams(vmem_limit_bytes=VMEM_LIMIT),
        cost_estimate=pl.CostEstimate(
            flops=64 * points * receivers * width * fl, bytes_accessed=4 * fl * receivers * width, transcendentals=0
        ),
        name="adjoint",
    )(turn, kernel, *ins)
    return out[:pieces], out[pieces:]


def forward_body(turn_ref, k_hbm, al_ref, init_ref, *refs, pieces, points, base, steps):
    d_refs, (o_ref, kbuf, sem, dscr, acc) = refs[:pieces], refs[pieces:]
    _, _, group, receivers, ts = kbuf.shape
    fl = k_hbm.shape[1]
    size = 2 * points * fl // pieces
    turn = turn_ref[0]
    acc[...] = jnp.zeros(acc.shape, F32)

    def step(s, n, block):
        tiles = range(ts // LANES)

        @pl.when(n == 0)
        def _():
            for k, d_ref in enumerate(d_refs):
                rows = pl.ds(pl.multiple_of((turn ^ k) * size, size), size)
                for j in tiles:
                    at = pl.ds(pl.multiple_of(s * ts + j * LANES, LANES), LANES)
                    dscr[j, rows, :] = d_ref[:, at].astype(F32)

        def part(c, f):
            rows = pl.ds(c * fl + n * group + f, points, stride=2 * fl)
            return jnp.concatenate([dscr[j, rows, :] for j in tiles], 1)

        field = jnp.concatenate([part(c, f) for f in range(group) for c in range(2)], 0).astype(BF16)
        acc[n] += lax.dot_general(
            field,
            block[...].reshape(2 * group * receivers, ts),
            (((1,), (1,)), ((), ())),
            preferred_element_type=F32,
        )

    stream(k_hbm, kbuf, sem, base, steps, step)
    for f in range(fl):
        n, g = divmod(f, group)
        whole = acc[n, 2 * points * g : 2 * points * (g + 1)]
        by_real = whole[:, g * receivers : (g + 1) * receivers]
        by_imag = whole[:, (group + g) * receivers : (group + g + 1) * receivers]
        top = 2 * points * f
        mid = top + points
        end = top + 2 * points
        real = by_real[:points] - by_imag[points:]
        imag = by_real[points:] + by_imag[:points]
        if init_ref is not None:
            real += init_ref[top:mid]
            imag += init_ref[mid:end]
        o_ref[top:mid] = real
        o_ref[mid:end] = imag
    extra = jnp.concatenate([al_ref[...], jnp.zeros((8, receivers - LANES), F32)], 1)
    if init_ref is not None:
        extra += init_ref[2 * points * fl :]
    o_ref[2 * points * fl :] = extra


def forward(turn, kernel, field, alignment, init, base):
    _, fl, receivers, sources = kernel.shape
    pieces = len(field)
    points = field[0].shape[0] * pieces // (2 * fl)
    width = field[0].shape[1]
    ts = tile_of(width, FORWARD_TILE)
    group = FORWARD_GROUP if fl % FORWARD_GROUP == 0 else 1
    depth = min(FORWARD_DEPTH, width // ts * fl // group)
    body = functools.partial(forward_body, pieces=pieces, points=points, base=base, steps=width // ts)
    if init is None:
        inner, start = body, []
        body = lambda turn, k, al, *rest: inner(turn, k, al, None, *rest)
    else:
        start = [init]
    specs = [pl.BlockSpec(memory_space=pltpu.SMEM), pl.BlockSpec(memory_space=pl.ANY), in_vmem()]
    return pl.pallas_call(
        body,
        in_specs=specs + [in_vmem()] * (len(start) + pieces),
        out_specs=in_vmem(),
        out_shape=jax.ShapeDtypeStruct((2 * points * fl + 8, receivers), F32),
        scratch_shapes=[
            pltpu.VMEM((depth, 2, group, receivers, ts), BF16),
            pltpu.SemaphoreType.DMA((depth,)),
            pltpu.VMEM((ts // LANES, 2 * points * fl + 2 * fl, LANES), F32),
            pltpu.VMEM((fl // group, 2 * points * group, 2 * receivers * group), F32),
        ],
        compiler_params=pltpu.CompilerParams(vmem_limit_bytes=VMEM_LIMIT),
        cost_estimate=pl.CostEstimate(
            flops=64 * points * receivers * width * fl, bytes_accessed=4 * fl * receivers * width, transcendentals=0
        ),
        name="forward",
    )(turn, kernel, alignment, *start, *field)


def split(whole):
    high = whole.astype(BF16)
    return high, (whole - high.astype(F32)).astype(BF16)


def taper_body(t_ref, *refs, inputs, points, rows):
    g_refs, d_refs, al_ref = refs[:inputs], refs[inputs:-1], refs[-1]
    width = g_refs[0].shape[1]
    step = tile_of(width, 512)
    own = len(d_refs) * rows
    total = jnp.zeros((8, LANES), F32)
    for p in range(points):
        high, low = split(t_ref[p])
        places = [
            (ref, slice(at, at + rows)) for ref in g_refs for at in range(p * rows, ref.shape[0], points * rows)
        ]
        for at in range(0, width, step):
            cols = slice(at, at + step)
            g = jnp.concatenate([ref[place, cols] for ref, place in places], 0)
            d = jnp.dot(low, g, preferred_element_type=F32)
            d += jnp.dot(high, g, preferred_element_type=F32)
            for k, ref in enumerate(d_refs):
                ref[p * rows : (p + 1) * rows, cols] = d[k * rows : (k + 1) * rows].astype(BF16)
            product = d * g[:own].astype(F32)
            for j in range(0, step, LANES):
                total += product[:, j : j + LANES].reshape(own // 8, 8, LANES).sum(0)
    al_ref[...] = total


def taper(matrices, blocks, outputs, rows):
    points = matrices.shape[0]
    width = blocks[0].shape[1]
    return pl.pallas_call(
        functools.partial(taper_body, inputs=len(blocks), points=points, rows=rows),
        in_specs=[in_vmem()] * (1 + len(blocks)),
        out_specs=[in_vmem()] * (outputs + 1),
        out_shape=[jax.ShapeDtypeStruct((points * rows, width), BF16)] * outputs
        + [jax.ShapeDtypeStruct((8, LANES), F32)],
        compiler_params=pltpu.CompilerParams(vmem_limit_bytes=VMEM_LIMIT),
        cost_estimate=pl.CostEstimate(
            flops=6 * matrices.size * width, bytes_accessed=8 * points * rows * outputs * width, transcendentals=0
        ),
        name="taper",
    )(matrices, *blocks)


def merge_body(own_ref, got_ref, p_ref, sums_ref):
    size, receivers = p_ref.shape
    projected = own_ref[:size] + got_ref[:size]
    p_ref[...] = projected
    squares = jnp.sum((projected * projected).reshape(size // 8, 8, receivers), 0)
    pad = -receivers % LANES
    if pad:
        squares = jnp.concatenate([squares, jnp.zeros((8, pad), F32)], 1)
    curvature = sum(squares[:, j : j + LANES] for j in range(0, receivers + pad, LANES))
    alignment = own_ref[size:, :LANES] + got_ref[size:, :LANES]
    both = jnp.concatenate([alignment[:4] + alignment[4:], curvature[:4] + curvature[4:]], 0)
    for at in range(0, sums_ref.shape[0], 8):
        sums_ref[at : at + 8] = both


def merge(own, got, count):
    size, receivers = own.shape
    return pl.pallas_call(
        merge_body,
        in_specs=[in_vmem()] * 2,
        out_specs=[in_vmem()] * 2,
        out_shape=[jax.ShapeDtypeStruct((size - 8, receivers), F32), jax.ShapeDtypeStruct((8 * count, LANES), F32)],
        name="merge",
    )(own, got)


def wave_table(freqs, fl):
    samples = np.arange(NT)[:, None]
    phase = (samples * np.arange(freqs)[None, :] % NT) * (2.0 * math.pi / NT)
    table = np.stack([np.cos(phase), -np.sin(phase)], 1) * freqs**-0.5
    table = table.reshape(NT, 2, freqs // fl, fl).transpose(0, 2, 1, 3)
    return table.reshape(NT, 2 * freqs).astype(np.float32)


def swap(x):
    return lax.ppermute(x, "src", [(0, 1), (1, 0)])


def step_length(s_ref):
    sums = sum(s_ref[at : at + 8] for at in range(0, s_ref.shape[0], 8))
    return jnp.sum(sums[0:4], keepdims=True) / jnp.sum(sums[4:8], keepdims=True)


def finish_body(place_ref, s_ref, p_ref, r_ref, *refs, spans, pieces):
    earlier, fields, (e_hbm, out_ref, stage, scr, sem) = refs[: ITERS - 1], refs[ITERS - 1 : -5], refs[-5:]
    _, fl, points, share = out_ref.shape
    lengths = [ref[0:1, 0:1] for ref in earlier] + [step_length(s_ref)]
    copies = []
    at = 0
    for part, ((base, width), count) in enumerate(zip(spans, pieces)):
        size = 2 * points * fl // count
        turn = place_ref[1 + part]

        def one(i, carry, at=at, base=base, count=count, size=size, turn=turn):
            off = pl.multiple_of(i * LANES, LANES)
            out = pl.ds(pl.multiple_of(base + i * LANES, LANES), LANES)
            for k in range(count):
                values = [fields[at + n * count + k][:, pl.ds(off, LANES)].astype(F32) for n in range(ITERS)]
                rows = pl.ds(pl.multiple_of((turn ^ k) * size, size), size)
                scr[i % 2, rows, :] = sum(a * x for a, x in zip(lengths, values))
            for c in range(2):
                for f in range(fl):
                    stage[c, f, :, out] = scr[i % 2, pl.ds(c * fl + f, points, stride=2 * fl), :]
            return carry

        lax.fori_loop(0, width // LANES, one, 0, unroll=4)
        span = pl.ds(base, width)
        copies.append(
            pltpu.make_async_copy(stage.at[:, :, :, span], e_hbm.at[:, :, :, span], sem.at[part])
        )
        copies[-1].start()
        at += ITERS * count
    for c in range(2):
        for f in range(fl):
            top = (2 * f + c) * points
            residual = r_ref[c, f] - lengths[-1] * p_ref[top : top + points]
            mine = residual[:, :share]
            for n in range(1, residual.shape[1] // share):
                mine = jnp.where(place_ref[0] == n, residual[:, n * share : (n + 1) * share], mine)
            out_ref[c, f] = mine
    for copy in copies:
        copy.wait()


def finish(core, turns, sums, projected, residual, lengths, fields, spans, fl, points, share):
    parts = range(len(spans))
    flat = [x for part in parts for field in fields for x in field[part]]
    shape = (2, fl, points, sum(width for _, width in spans))
    return pl.pallas_call(
        functools.partial(finish_body, spans=spans, pieces=[len(fields[0][part]) for part in parts]),
        in_specs=[pl.BlockSpec(memory_space=pltpu.SMEM)] + [in_vmem()] * (3 + len(lengths) + len(flat)),
        out_specs=[pl.BlockSpec(memory_space=pl.ANY), in_vmem()],
        out_shape=[jax.ShapeDtypeStruct(shape, F32), jax.ShapeDtypeStruct((2, fl, points, share), F32)],
        scratch_shapes=[
            pltpu.VMEM(shape, F32),
            pltpu.VMEM((2, 2 * points * fl + 2 * fl, LANES), F32),
            pltpu.SemaphoreType.DMA((len(spans),)),
        ],
        compiler_params=pltpu.CompilerParams(vmem_limit_bytes=VMEM_LIMIT),
        name="finish",
    )(jnp.concatenate([core] + turns), sums, projected, residual, *lengths, *flat)


def then(x, *earlier):
    return lax.optimization_barrier((x, *earlier))[0]


def send(x, hop):
    return lax.ppermute(x, "freq", [(i, i ^ hop) for i in range(lax.axis_size("freq"))])


def exchange(x, rows):
    width = x.shape[-1]
    return lax.all_to_all(x.reshape(-1, rows, width), "freq", 0, 0, tiled=True).reshape(-1, width)


def body(kernel, data, win_start, win_end):
    count = lax.axis_size("freq")
    src_count = lax.axis_size("src")
    _, fl, receivers, sources = kernel.shape
    points = data.shape[3]
    rows = 2 * fl
    me = lax.axis_index("freq")
    own = points // count
    permutes = count & (count - 1) == 0 and rows % 16 == 0 and own == 1
    inner = {"plain": 1, "direct": 1, "relay": 2}
    parts, base = [], 0
    for weight, mode in PARTS:
        width = sources * weight // sum(w for w, _ in PARTS)
        parts.append((base, width, mode if permutes else "plain"))
        base += width

    def turn_of(mode):
        turn = (me // inner[mode]).reshape(1).astype(jnp.int32)
        return jnp.zeros_like(turn) if mode == "plain" else turn

    def pieces_of(mode):
        return 1 if mode == "plain" else count // inner[mode]

    table = jnp.asarray(wave_table(fl * count, fl))
    samples = jnp.arange(NT, dtype=jnp.int32)[None, :]

    def matrices_of(mode):
        size = own * inner[mode]
        first = me // inner[mode] * size
        starts = lax.dynamic_slice_in_dim(win_start, first, size)[:, None]
        ends = lax.dynamic_slice_in_dim(win_end, first, size)[:, None]
        window = ((samples >= starts) & (samples < ends)).astype(F32)
        right = table
        if mode != "plain":
            blocks = table.reshape(NT, count, rows)
            order = [me ^ (k * inner[mode] + y) for y in range(inner[mode]) for k in range(pieces_of(mode))]
            right = jnp.concatenate([lax.dynamic_index_in_dim(blocks, b, 1, keepdims=False) for b in order], 1)
        left = right[:, : right.shape[1] // inner[mode]]
        return jnp.einsum("pta,tb->pab", window[:, :, None] * left, right, precision=lax.Precision.HIGHEST)

    matrices = {mode: matrices_of(mode) for mode in sorted({mode for _, _, mode in parts})}

    def scatter(blocks, mode):
        if mode == "plain":
            return [exchange(blocks[0], rows)]
        return [blocks[0]] + [send(blocks[k], k * inner[mode]) for k in range(1, len(blocks))]

    def pair_up(got, mode):
        if mode != "relay":
            return got
        joined = jnp.concatenate(got, 0)
        return [joined, send(joined, 1)]

    def tapered(got, mode):
        if mode != "plain":
            *field, alignment = taper(matrices[mode], got, pieces_of(mode), rows)
            return field, alignment
        if own == 1:
            field, alignment = taper(matrices[mode], got, 1, count * rows)
            return [field], alignment
        width = got[0].shape[-1]
        got = got[0].reshape(count, own, rows, width)
        done = [
            taper(matrices[mode][p : p + 1], [got[:, p].reshape(-1, width)], 1, count * rows) for p in range(own)
        ]
        field = jnp.stack([d.reshape(count, rows, width) for d, _ in done], 1).reshape(-1, width)
        return [field], sum(a for _, a in done)

    residual = data.transpose(0, 1, 3, 2)
    lengths, fields = [], []
    for iteration in range(ITERS):
        image = None
        fields.append([])
        gradients, gathered, sent = [], [], []
        if iteration == 0:
            stage, ins = "data", [residual]
        else:
            stage, ins = "step", [residual, sums, projected]
        for base, width, mode in parts:
            gradient, made = adjoint(turn_of(mode), kernel, ins, stage, points, base, width, pieces_of(mode))
            if stage == "step":
                residual = made[1]
                lengths.append(made[2])
            if made:
                lhs = made[0]
            stage, ins = "rest", [then(lhs, gradient[-1])]
            gradients.append(gradient)
            if gathered and mode == "relay":
                gradient = list(gradient[:2]) + [then(x, gathered[-1][0]) for x in gradient[2:3]] + list(gradient[3:])
            gathered.append(pair_up(scatter(gradient, mode), mode))
        for n, (_, _, mode) in enumerate(parts):
            got = gathered[n]
            if n + 1 < len(parts):
                got = [then(got[0], gradients[n + 1][-1])] + got[1:]
            field, alignment = tapered(got, mode)
            if sent and mode == "relay":
                field = list(field[:2]) + [then(x, sent[-1][1][len(field) // 2]) for x in field[2:]]
            sent.append((field, scatter(field, mode), alignment))
        for n, (base, _, mode) in enumerate(parts):
            _, field, alignment = sent[n]
            if n + 1 < len(parts):
                field = [then(field[0], sent[n + 1][0][-1])] + field[1:]
            image = forward(turn_of(mode), kernel, field, alignment, image, base)
            fields[-1].append(field)
        got = swap(image) if src_count == 2 else lax.psum(image, "src") - image
        projected, sums = merge(image, got, count)
        sums = exchange(sums, 8)
    spans = [(base, width) for base, width, _ in parts]
    turns = [turn_of(mode) for _, _, mode in parts]
    core = lax.axis_index("src").reshape(1).astype(jnp.int32)
    share = receivers // src_count
    estimate, residual = finish(
        core, turns, sums, projected, residual, lengths, fields, spans, fl, points, share
    )
    return estimate, residual.transpose(0, 1, 3, 2)


def solution(mesh):
    in_specs = (P("grp", "freq", None, "src"), P("grp", "freq", None, None), P("grp"), P("grp"))
    out_specs = (P("grp", "freq", None, "src"), P("grp", "freq", "src", None))
    return jax.shard_map(body, mesh=mesh, in_specs=in_specs, out_specs=out_specs, check_vma=False)
```
